128 devices in a mesh: dp: 8 (over y_hi, z), owner: 16 (over y_lo, x, core).
Axes of the slice: x: 4, y: 4 (y_hi: 2, y_lo: 2; y = y_hi * 2 + y_lo), z: 4, core: 2. Of those that a mesh axis runs over, the one named last changes fastest.
Arguments:
- activations: bfloat16 [6144, 6144], P('dp', 'owner'), may hold values from -6 to 6
- out_grads: bfloat16 [6144, 6144], P('dp'), may hold values from -0.078125 to 0.078125
- basis_in: bfloat16 [6144, 6144], P('owner'), may hold values from -0.078125 to 0.078125
- basis_out: bfloat16 [6144, 6144], P(None, 'owner'), may hold values from -0.078125 to 0.078125
- eig_in: float32 [6144], replicated, may hold values from 0.3 to 3
- eig_out: float32 [6144], replicated, may hold values from 0.3 to 3
Outputs:
- precond: bfloat16 [6144, 6144], P(None, 'owner')
The draws below stay inside these ranges and needn't reach their ends.
All inputs are finite; a program needn't handle non-finite values.
Results may differ from the reference program's by a relative error of at most 0.03.
Values may be sent and summed in bfloat16 or wider, within the bound.
A program may use at most 128 MiB of HBM per device.

```python
import math
import jax
import jax.numpy as jnp
from jax import lax

IN = 6144
OUT = 6144
TOK = 768
TOKENS = 6144
N_DP = 8


def block_scale(rng, shape, pieces, low, largest):
    def one(position, parts):
        heights = jax.random.uniform(jax.random.fold_in(jax.random.fold_in(rng, 6), position), (parts,), jnp.float32, low / len(pieces), largest / len(pieces))
        return jnp.repeat(jnp.exp(heights), shape[position] // parts).reshape((-1,) + (1,) * (len(shape) - position - 1))

    gain = one(*pieces[0])
    for cut in pieces[1:]:
        gain = gain * one(*cut)
    return gain


def noise(key, shape, spread, most, pieces=(), held_as=jnp.bfloat16):
    values = spread * jax.random.normal(key, shape, jnp.float32)
    if pieces:
        values = values * block_scale(key, shape, pieces, -0.22, 0.18)
    return jnp.clip(values, -most, most).astype(held_as)


def setup_inputs(seed: int = 0) -> dict:
    streams_of = jax.random.split(jax.random.key(seed), 7)
    activations = noise(streams_of[0], (TOKENS, IN), 1.0, 6.0, ((0, 8), (1, 16)))
    out_grads = noise(streams_of[1], (TOKENS, OUT), TOKENS ** -0.5, 0.078125, ((0, 8),))
    basis_in = noise(streams_of[2], (IN, IN), IN ** -0.5, 0.078125, ((0, 16),))
    basis_out = noise(streams_of[3], (OUT, OUT), OUT ** -0.5, 0.078125, ((1, 16),))
    eig_in = jnp.clip(jnp.exp(jax.random.uniform(streams_of[4], (IN,), jnp.float32, math.log(0.3), math.log(3.0))), 0.3, 3.0)
    eig_out = jnp.clip(jnp.exp(jax.random.uniform(streams_of[5], (OUT,), jnp.float32, math.log(0.3), math.log(3.0))), 0.3, 3.0)
    return {"activations": activations, "out_grads": out_grads, "basis_in": basis_in, "basis_out": basis_out, "eig_in": eig_in, "eig_out": eig_out}


damping = 0.1


def reference(activations, out_grads, basis_in, basis_out, eig_in, eig_out):
    gradient = jnp.zeros((IN, OUT), jnp.float32)
    for replica in range(N_DP):
        token_acts = activations[replica * TOK:(replica + 1) * TOK]
        token_grads = out_grads[replica * TOK:(replica + 1) * TOK]
        partial_value = jnp.dot(token_acts.T, token_grads, preferred_element_type=jnp.float32).astype(jnp.bfloat16)
        partial_value = lax.optimization_barrier(partial_value)
        gradient = gradient + partial_value.astype(jnp.float32)
    gradient = gradient.astype(jnp.bfloat16)
    rot_left = jnp.dot(basis_in, gradient, preferred_element_type=jnp.float32).astype(jnp.bfloat16)
    product = jnp.dot(rot_left, basis_out, preferred_element_type=jnp.float32)
    scaled = (product / (eig_in[:, None] * eig_out[None, :] + damping)).astype(jnp.bfloat16)
    rot_back = jnp.dot(scaled, basis_out.T, preferred_element_type=jnp.float32).astype(jnp.bfloat16)
    return jnp.dot(basis_in.T, rot_back, preferred_element_type=jnp.float32).astype(jnp.bfloat16)
```

```python
import jax
import jax.numpy as jnp
from jax import lax
from jax.experimental import pallas as pl
from jax.experimental.pallas import tpu as pltpu
from jax.sharding import PartitionSpec as P

damping = 0.1
bf16 = jnp.bfloat16
f32 = jnp.float32
MESH = pl.DeviceIdType.MESH


def device(yh, z, yl, x, c):
    return (yh * 4 + z, yl * 8 + x * 2 + c)


def visit(s, p, q):
    k = s % 3
    last = s // 6
    dq = (1 - last) * (k * (k + 1) // 2) + 2 * last
    dp = (1 - last) * (s // 3) + last * k
    return (p + dp) % 2, (q + dq) % 4


class Gather:
    def __init__(self, part, ssem, rsem, p, q, to):
        self.part, self.ssem, self.rsem, self.p, self.q, self.to = part, ssem, rsem, p, q, to

    def copy(self, k):
        p, q = self.p, self.q
        o, r, l = 1 - p, (q + 1) % 4, (q + 3) % 4
        pp, qq, half, dest = (
            (p, q, None, (o, q)),
            (p, q, None, (p, r)),
            (p, q, None, (p, l)),
            (o, q, None, (p, r)),
            (o, q, None, (p, l)),
            (p, l, 0, (p, r)),
            (p, r, 1, (p, l)),
            (o, l, 0, (p, r)),
            (o, r, 1, (p, l)),
        )[k]
        ref = self.part(pp * 4 + qq, half)
        return pltpu.make_async_remote_copy(
            ref, ref, self.ssem.at[k], self.rsem.at[k], device_id=self.to(*dest), device_id_type=MESH
        )

    def start(self, *ks):
        for k in ks:
            self.copy(k).start()

    def got(self, *ks):
        p, q = self.p, self.q
        o, r, l, a = 1 - p, (q + 1) % 4, (q + 3) % 4, (q + 2) % 4
        for k in ks:
            pp, qq, half = (
                (o, q, None), (p, l, None), (p, r, None), (o, l, None), (o, r, None),
                (p, a, 0), (p, a, 1), (o, a, 0), (o, a, 1),
            )[k]
            ref = self.part(pp * 4 + qq, half)
            pltpu.make_async_remote_copy(
                ref, ref, self.ssem.at[k], self.rsem.at[k], device_id=self.to(o, q), device_id_type=MESH
            ).wait_recv()

    def first(self):
        self.start(0, 1, 2)

    def second(self):
        self.got(0)
        self.start(3, 4)
        self.got(1)
        self.start(5)
        self.got(2)
        self.start(6)

    def third(self):
        self.got(3)
        self.start(7)
        self.got(4)
        self.start(8)

    def sent(self):
        for k in range(9):
            self.copy(k).wait_send()


def kernel(
    at_ref, g_ref, bi_ref, bo_ref, ein_ref, eout_ref, o_ref,
    ag, ym, zp, zbuf, zsend, zy, zfull, big, pp, pbuf, psend, py, sc, bo,
    wbuf, wsend, wy, wg, acc, frecv,
    lsem, gsem, bsem, tsem, osem,
    a_s, a_r, b_s, b_r, w_s, w_r, o_s, o_r,
    z_s, z_r, zy_s, zy_r, p_s, p_r, py_s, py_r, x_s, x_r, xy_s, xy_r, sib_s, sib_r,
):
    rep = lax.axis_index("dp")
    own = lax.axis_index("owner")
    yh, z = rep // 4, rep % 4
    yl, x, c = own // 8, (own // 2) % 4, own % 2
    m = yl * 4 + x
    oc = 1 - c

    def remote(src, dst, s, r, dest):
        return pltpu.make_async_remote_copy(src, dst, s, r, device_id=dest, device_id_type=MESH)

    sibling = device(yh, z, yl, x, oc)
    ypair = device(1 - yh, z, yl, x, c)
    lpair = device(yh, z, 1 - yl, x, c)
    over_owner = lambda p, q: device(yh, z, p, q, c)
    over_dp = lambda p, q: device(p, q, yl, x, c)

    barrier = pltpu.get_barrier_semaphore()
    partners = [sibling, ypair, lpair]
    partners += [over_owner(yl, (x + d) % 4) for d in (1, 2, 3)]
    partners += [over_dp(yh, (z + d) % 4) for d in (1, 2, 3)]
    for dest in partners:
        pl.semaphore_signal(barrier, inc=1, device_id=dest, device_id_type=MESH)

    def bo_chunk(k):
        rows = pl.ds(pl.multiple_of(k * 768, 768), 768)
        return pltpu.make_async_copy(bo_ref.at[rows], bo.at[c, rows], bsem.at[k])

    def g_half(k, h):
        cols = pl.ds(pl.multiple_of(k * 768, 768), 768)
        return pltpu.make_async_copy(
            g_ref.at[pl.ds(h * 384, 384), cols], zp.at[2 * (k % 4) + h], gsem.at[k % 4, h]
        )

    def tile_start(q, core):
        return pl.multiple_of(((2 * (q // 3) + core) * 3 + q % 3) * 128, 128)

    def bi_tile(j):
        dst = big.at[m, :, :, pl.ds(j * 128, 128)]
        return pltpu.make_async_copy(
            bi_ref.at[:, :, pl.ds(tile_start(rep + 8 * (j % 3), j // 3), 128)], dst, tsem.at[j]
        )

    load_a = pltpu.make_async_copy(at_ref, ag.at[m], lsem.at[0])
    load_a.start()
    for k in range(8):
        bo_chunk(k).start()
        if k < 4:
            g_half(k, 0).start()
            g_half(k, 1).start()
    for j in range(6):
        bi_tile(j).start()

    gather_a = Gather(
        lambda slot, h: ag.at[slot] if h is None else ag.at[slot, pl.ds(h * 192, 192)],
        a_s, a_r, yl, x, over_owner,
    )
    gather_b = Gather(
        lambda slot, h: big.at[slot] if h is None else big.at[slot, pl.ds(h * 4, 4)],
        b_s, b_r, yl, x, over_owner,
    )
    gather_w = Gather(
        lambda slot, h: wg.at[slot] if h is None else wg.at[slot, pl.ds(h * 192, 192)],
        w_s, w_r, yh, z, over_dp,
    )
    gather_o = Gather(
        lambda slot, h: ag.at[slot] if h is None else ag.at[slot, pl.ds(h * 192, 192)],
        o_s, o_r, yh, z, over_dp,
    )

    load_a.wait()
    pl.semaphore_wait(barrier, len(partners))
    gather_a.first()
    send_bo = remote(bo_ref, bo.at[c], sib_s.at[0], sib_r.at[0], sibling)
    send_bo.start()

    half = pl.ds(0, 384)
    acc[:, half] = jnp.zeros((768, 384), f32)

    @pl.loop(0, 8)
    def _(k):
        bo_chunk(k).wait()
        g_half(k, 0).wait()
        g_half(k, 1).wait()
        rows = pl.ds(pl.multiple_of(k * 768, 768), 768)
        part = zp[pl.ds(2 * (k % 4), 2)].reshape(768, 768)
        acc[:, half] += jnp.dot(part, bo[c, rows, :], preferred_element_type=f32)

        @pl.when(k < 4)
        def _():
            g_half(k + 4, 0).start()
            g_half(k + 4, 1).start()

    mine = pl.ds(pl.multiple_of(c * 384, 128), 384)
    other = pl.ds(pl.multiple_of(oc * 384, 128), 384)
    ym[:, mine] = acc[:, half].astype(bf16)
    send_y = remote(ym.at[:, mine], ym.at[:, mine], sib_s.at[1], sib_r.at[1], sibling)
    send_y.start()
    remote(ym.at[:, other], ym.at[:, other], sib_s.at[1], sib_r.at[1], sibling).wait_recv()

    def z_part(q):
        return zp.at[q // 3, pl.ds(pl.multiple_of((q % 3) * 128, 128), 128)]

    def z_copy(yt, i, dz):
        zt = (z + dz) % 4
        j = yt * 3 + i
        return remote(
            z_part(yt * 4 + zt + 8 * i), zbuf.at[dz - 1, j], z_s.at[dz - 1, j], z_r.at[dz - 1, j], over_dp(yh, zt)
        )

    @pl.loop(0, 8)
    def _(s):
        @pl.when(s == 1)
        def _():
            gather_a.second()

        @pl.when(s == 4)
        def _():
            gather_a.third()

        @pl.when(s == 6)
        def _():
            gather_a.got(5, 6)
            for j in range(6):
                bi_tile(j).wait()
            gather_b.first()

        @pl.when(s == 7)
        def _():
            gather_a.got(7, 8)

        p_, q_ = visit(s, yl, x)
        blk = p_ * 4 + q_
        zp[blk] = jnp.dot(ag[blk], ym[...], preferred_element_type=f32).astype(bf16)

        @pl.loop(0, 3)
        def _(t):
            q = 3 * blk + t
            r_, i = q % 8, q // 8
            dz = (r_ % 4 + 4 - z) % 4

            @pl.when(dz != 0)
            def _():
                z_copy(r_ // 4, i, dz).start()

    gather_a.sent()
    gather_b.second()

    def z_sum(yt, i):
        j = yt * 3 + i
        total = z_part(yt * 4 + z + 8 * i)[...].astype(f32)
        for d in range(3):
            remote(zbuf.at[d, j], zbuf.at[d, j], z_s.at[d, j], z_r.at[d, j], ypair).wait_recv()
            total = total + zbuf[d, j].astype(f32)
        return total

    def zy_copy(i):
        return remote(zsend.at[i], zy.at[i], zy_s.at[i], zy_r.at[i], ypair)

    @pl.loop(0, 3)
    def _(i):
        zsend[i] = z_sum(1 - yh, i).astype(bf16)
        zy_copy(i).start()

    def z_rows(core):
        return zfull.at[pl.ds(pl.multiple_of(core * 384, 128), 384)]

    @pl.loop(0, 3)
    def _(i):
        total = z_sum(yh, i)
        zy_copy(i).wait()
        total = total + zy[i].astype(f32)
        zfull[pl.ds(pl.multiple_of(c * 384 + i * 128, 128), 128), :] = total.astype(bf16)

    send_z = remote(z_rows(c), z_rows(c), sib_s.at[2], sib_r.at[2], sibling)
    send_z.start()
    gather_b.third()
    remote(z_rows(oc), z_rows(oc), sib_s.at[2], sib_r.at[2], sibling).wait_recv()

    def p_copy(blk, dz):
        zt = (z + dz) % 4
        return remote(
            pp.at[blk, pl.ds(zt * 2, 2)], pbuf.at[dz - 1, blk], p_s.at[dz - 1, blk], p_r.at[dz - 1, blk],
            over_dp(yh, zt),
        )

    @pl.loop(0, 8)
    def _(s):
        @pl.when(s == 6)
        def _():
            gather_b.got(5, 6)

        @pl.when(s == 7)
        def _():
            gather_b.got(7, 8)

        p_, q_ = visit(s, yl, x)
        blk = p_ * 4 + q_
        part = jnp.dot(big[blk].reshape(384, 768), zfull[...], preferred_element_type=f32)
        pp[blk] = part.astype(bf16).reshape(8, 48, 768)
        for dz in (1, 2, 3):
            p_copy(blk, dz).start()

    gather_b.sent()

    @pl.loop(0, 6)
    def _(j):
        for dz in (1, 2, 3):
            z_copy(j // 3, j % 3, dz).wait_send()

    def p_sum(blk, h):
        total = pp[blk, 2 * z + h].astype(f32)
        for d in range(3):
            total = total + pbuf[d, blk, h].astype(f32)
        return total

    def py_copy(blk):
        return remote(psend.at[blk], py.at[blk], py_s.at[blk], py_r.at[blk], ypair)

    @pl.loop(0, 8)
    def _(s):
        p_, q_ = visit(s, yl, x)
        blk = p_ * 4 + q_
        for d in range(3):
            remote(pbuf.at[d, blk], pbuf.at[d, blk], p_s.at[d, blk], p_r.at[d, blk], ypair).wait_recv()
        psend[blk] = p_sum(blk, 1 - yh).astype(bf16)
        py_copy(blk).start()

    @pl.loop(0, 8)
    def _(s):
        p_, q_ = visit(s, yl, x)
        blk = p_ * 4 + q_
        py_copy(blk).wait()
        total = p_sum(blk, yh) + py[blk].astype(f32)
        scale = ein_ref[blk] * eout_ref[pl.ds(m, 1), :] + damping
        sc[blk] = (total / scale).astype(bf16)
        for dz in (1, 2, 3):
            p_copy(blk, dz).wait_send()

    remote(bo_ref, bo.at[oc], sib_s.at[0], sib_r.at[0], sibling).wait_recv()
    nt = (((1,), (1,)), ((), ()))

    def w_copy(dx, yt):
        xt = (x + dx) % 4
        j = (dx - 1) * 2 + yt
        return remote(zp.at[yt * 4 + xt], wbuf.at[j], x_s.at[j], x_r.at[j], over_owner(yl, xt))

    @pl.loop(0, 8)
    def _(s):
        dx, yt = (s // 2 + 1) % 4, s % 2
        blk = yt * 4 + (x + dx) % 4
        rows = pl.ds(pl.multiple_of(blk * 768, 768), 768)
        lhs = sc[...].reshape(384, 768)
        part = lax.dot_general(lhs[:, :384], bo[0, rows, :], nt, preferred_element_type=f32)
        part += lax.dot_general(lhs[:, 384:], bo[1, rows, :], nt, preferred_element_type=f32)
        zp[blk] = part.astype(bf16)

        @pl.when(dx != 0)
        def _():
            w_copy(dx, yt).start()

    def w_got(yt):
        for d in range(3):
            j = d * 2 + yt
            remote(wbuf.at[j], wbuf.at[j], x_s.at[j], x_r.at[j], lpair).wait_recv()

    def w_sum(yt, rows):
        total = zp[yt * 4 + x, rows].astype(f32)
        for d in range(3):
            total = total + wbuf[d * 2 + yt, rows].astype(f32)
        return total

    def wy_copy(i):
        return remote(wsend.at[i], wy.at[i], xy_s.at[i], xy_r.at[i], lpair)

    w_got(1 - yl)

    @pl.loop(0, 3)
    def _(i):
        wsend[i] = w_sum(1 - yl, pl.ds(pl.multiple_of(i * 128, 128), 128)).astype(bf16)
        wy_copy(i).start()

    w_got(yl)

    @pl.loop(0, 3)
    def _(i):
        rows = pl.ds(pl.multiple_of(i * 128, 128), 128)
        total = w_sum(yl, rows)
        wy_copy(i).wait()
        wg[rep, rows] = (total + wy[i].astype(f32)).astype(bf16)

    @pl.loop(0, 3)
    def _(d):
        for yt in range(2):
            w_copy(d + 1, yt).wait_send()

    gather_w.first()
    acc[...] = jnp.zeros_like(acc)

    @pl.loop(0, 8)
    def _(s):
        @pl.when(s == 1)
        def _():
            gather_w.second()

        @pl.when(s == 4)
        def _():
            gather_w.third()

        @pl.when(s == 6)
        def _():
            gather_w.got(5, 6)

        @pl.when(s == 7)
        def _():
            gather_w.got(7, 8)

        p_, q_ = visit(s, yh, z)
        lhs = big[:, q_ * 2 + p_].reshape(384, 768)
        acc[...] += lax.dot_general(
            lhs, wg[p_ * 4 + q_], (((0,), (0,)), ((), ())), preferred_element_type=f32
        )

    gather_w.sent()
    send_f = remote(acc.at[:, other], frecv, sib_s.at[3], sib_r.at[3], sibling)
    send_f.start()
    remote(frecv, frecv, sib_s.at[3], sib_r.at[3], sibling).wait_recv()
    for core in range(2):
        rows = pl.ds(core * 384, 384)
        ag[rep, :, pl.ds(core * 384, 384)] = (acc[rows, mine] + frecv[rows, :]).astype(bf16)

    gather_o.first()

    def store(r_, j):
        src = ag.at[r_, pl.ds((j % 3) * 128, 128), pl.ds((j // 3) * 384, 384)]
        dst = o_ref.at[pl.ds(tile_start(r_ + 8 * (j % 3), j // 3), 128)]
        return pltpu.make_async_copy(src, dst, osem.at[r_, j])

    @pl.loop(0, 8)
    def _(s):
        @pl.when(s == 1)
        def _():
            gather_o.second()

        @pl.when(s == 4)
        def _():
            gather_o.third()

        @pl.when(s == 6)
        def _():
            gather_o.got(5, 6)

        @pl.when(s == 7)
        def _():
            gather_o.got(7, 8)

        p_, q_ = visit(s, yh, z)
        for j in range(6):
            store(p_ * 4 + q_, j).start()

    gather_o.sent()
    send_bo.wait_send()
    send_y.wait_send()
    send_z.wait_send()
    send_f.wait_send()

    @pl.loop(0, 8)
    def _(r_):
        for j in range(6):
            store(r_, j).wait()


def shards(activations, out_grads, basis_in, basis_out, eig_in, eig_out):
    rep = lax.axis_index("dp")
    core = lax.axis_index("owner") % 2
    sub = (rep % 4) * 2 + rep // 4
    ein = lax.dynamic_slice(eig_in.reshape(8, 2, 8, 48), (0, core, sub, 0), (8, 1, 1, 48)).reshape(8, 48, 1)
    dma = pltpu.SemaphoreType.DMA
    v = pltpu.VMEM
    scratch = [
        v((8, 384, 768), bf16), v((768, 768), bf16), v((8, 384, 768), bf16), v((3, 6, 128, 768), bf16),
        v((3, 128, 768), bf16), v((3, 128, 768), bf16), v((768, 768), bf16), v((8, 8, 48, 768), bf16),
        v((8, 8, 48, 768), bf16), v((3, 8, 2, 48, 768), bf16), v((8, 48, 768), bf16), v((8, 48, 768), bf16),
        v((8, 48, 768), bf16), v((2, 6144, 384), bf16),
        v((6, 384, 768), bf16), v((3, 128, 768), bf16), v((3, 128, 768), bf16), v((8, 384, 768), bf16),
        v((768, 768), f32), v((768, 384), f32),
        dma((1,)), dma((4, 2)), dma((8,)), dma((6,)), dma((8, 6)),
    ]
    scratch += [dma((9,))] * 8
    scratch += [dma((3, 6))] * 2 + [dma((3,))] * 2 + [dma((3, 8))] * 2 + [dma((8,))] * 2
    scratch += [dma((6,))] * 2 + [dma((3,))] * 2 + [dma((4,))] * 2
    hbm = pl.BlockSpec(memory_space=pl.ANY)
    vmem = pl.BlockSpec(memory_space=pltpu.VMEM)
    return pl.pallas_call(
        kernel,
        out_shape=jax.ShapeDtypeStruct((6144, 384), bf16),
        in_specs=[hbm, hbm, hbm, hbm, vmem, vmem],
        out_specs=hbm,
        scratch_shapes=scratch,
        compiler_params=pltpu.CompilerParams(
            collective_id=0, has_side_effects=True, vmem_limit_bytes=63 * 2**20
        ),
        name="precondition",
    )(
        activations.T, out_grads, basis_in.reshape(8, 48, 6144), basis_out, ein, eig_out.reshape(8, 768)
    )


def solution(mesh):
    in_specs = (P("dp", "owner"), P("dp", None), P("owner", None), P(None, "owner"), P(), P())
    out_specs = P(None, "owner")
    return jax.shard_map(shards, mesh=mesh, in_specs=in_specs, out_specs=out_specs, check_vma=False)
```

```python
import jax
import jax.numpy as jnp
from jax import lax
from jax.experimental import pallas as pl
from jax.experimental.pallas import tpu as pltpu
from jax.sharding import PartitionSpec as P

damping = 0.1
bf16 = jnp.bfloat16
f32 = jnp.float32
MESH = pl.DeviceIdType.MESH
parts = 3


def device(yh, z, yl, x, c):
    return (yh * 4 + z, yl * 8 + x * 2 + c)


def remote(src, dst, s, r, dest):
    return pltpu.make_async_remote_copy(src, dst, s, r, device_id=dest, device_id_type=MESH)


class Gather:
    def __init__(self, part, ssem, rsem, p, q, to):
        self.part, self.ssem, self.rsem, self.p, self.q, self.to = part, ssem, rsem, p, q, to

    def copy(self, j, k):
        p, q = self.p, self.q
        o, r, l = 1 - p, (q + 1) % 4, (q + 3) % 4
        pp, qq, half, dest = (
            (p, q, None, (o, q)),
            (p, q, None, (p, r)),
            (p, q, None, (p, l)),
            (o, q, None, (p, r)),
            (o, q, None, (p, l)),
            (p, l, 0, (p, r)),
            (p, r, 1, (p, l)),
            (o, l, 0, (p, r)),
            (o, r, 1, (p, l)),
        )[k]
        ref = self.part(j, pp, qq, half)
        return remote(ref, ref, self.ssem.at[j, k], self.rsem.at[j, k], self.to(*dest))

    def start(self, j, *ks):
        for k in ks:
            self.copy(j, k).start()

    def got(self, j, *ks):
        p, q = self.p, self.q
        o, r, l, a = 1 - p, (q + 1) % 4, (q + 3) % 4, (q + 2) % 4
        for k in ks:
            pp, qq, half = (
                (o, q, None), (p, l, None), (p, r, None), (o, l, None), (o, r, None),
                (p, a, 0), (p, a, 1), (o, a, 0), (o, a, 1),
            )[k]
            ref = self.part(j, pp, qq, half)
            remote(ref, ref, self.ssem.at[j, k], self.rsem.at[j, k], self.to(o, q)).wait_recv()

    def first(self, j):
        self.start(j, 0, 1, 2)

    def second(self, j):
        self.got(j, 0)
        self.start(j, 3, 4)
        self.got(j, 1)
        self.start(j, 5)
        self.got(j, 2)
        self.start(j, 6)

    def third(self, j):
        self.got(j, 3)
        self.start(j, 7)
        self.got(j, 4)
        self.start(j, 8)

    def last(self, j):
        self.got(j, 5, 6, 7, 8)

    def sent(self, j):
        for k in range(9):
            self.copy(j, k).wait_send()


class Reduce:
    def __init__(self, src, bufs, sems, p, q, to):
        self.src, self.p, self.q, self.to = src, p, q, to
        self.mid, self.end, self.out, self.got = bufs
        self.ssem, self.rsem, self.psem, self.qsem = sems

    def copy(self, j, k):
        q = self.q
        r, l, a = (q + 1) % 4, (q + 3) % 4, (q + 2) % 4
        right, left = self.to(self.p, r), self.to(self.p, l)
        src, dst, dest = (
            (self.src.at[j, a, 0], self.mid.at[j, 0], right),
            (self.src.at[j, a, 1], self.mid.at[j, 1], left),
            (self.src.at[j, r, 1], self.end.at[j, 0, 1], right),
            (self.src.at[j, l, 0], self.end.at[j, 1, 0], left),
            (self.src.at[j, r, 0], self.end.at[j, 0, 0], right),
            (self.src.at[j, l, 1], self.end.at[j, 1, 1], left),
        )[k]
        return remote(src, dst, self.ssem.at[j, k], self.rsem.at[j, k], dest)

    def pair(self, j):
        return remote(
            self.out.at[j], self.got.at[j], self.psem.at[j], self.qsem.at[j], self.to(1 - self.p, self.q)
        )

    def far(self, j):
        self.copy(j, 0).start()
        self.copy(j, 1).start()

    def near(self, j):
        self.copy(j, 2).start()
        self.copy(j, 3).start()

    def merge(self, j):
        for h in range(2):
            t = (self.q + 1 + 2 * h) % 4
            self.copy(j, h).wait_recv()
            self.src[j, t, h] = (self.src[j, t, h].astype(f32) + self.mid[j, h].astype(f32)).astype(bf16)
            self.copy(j, 4 + h).start()

    def total(self, j, h):
        return (
            self.src[j, self.q, h].astype(f32) + self.end[j, 0, h].astype(f32) + self.end[j, 1, h].astype(f32)
        )

    def swap(self, j):
        for k in range(2, 6):
            self.copy(j, k).wait_recv()
        self.out[j] = self.total(j, 1 - self.p).astype(bf16)
        self.pair(j).start()

    def result(self, j):
        self.pair(j).wait_recv()
        return self.total(j, self.p) + self.got[j].astype(f32)

    def sent(self, j):
        for k in range(6):
            self.copy(j, k).wait_send()
        self.pair(j).wait_send()


def kernel(
    at_ref, g_ref, bi_ref, bo_ref, ein_ref, eout_ref, o_ref,
    ag, ym, zp, zfull, big, pp, sc, bo, wg, acc, frecv, outg,
    z1, z2, z3, z4, p1, p2, p3, p4, w1, w2, w3, w4,
    lsem, gsem, bsem, tsem, osem,
    a_s, a_r, b_s, b_r, w_s, w_r, o_s, o_r,
    zs, zr, zps, zpr, ps, pr, pps, ppr, xs, xr, xps, xpr, sib_s, sib_r,
):
    rep = lax.axis_index("dp")
    own = lax.axis_index("owner")
    yh, z = rep // 4, rep % 4
    yl, x, c = own // 8, (own // 2) % 4, own % 2
    m = yl * 4 + x
    oc = 1 - c

    sibling = device(yh, z, yl, x, oc)
    over_owner = lambda p, q: device(yh, z, p, q, c)
    over_dp = lambda p, q: device(p, q, yl, x, c)

    barrier = pltpu.get_barrier_semaphore()
    partners = [sibling, over_dp(1 - yh, z), over_owner(1 - yl, x)]
    partners += [over_owner(yl, (x + d) % 4) for d in (1, 3)]
    partners += [over_dp(yh, (z + d) % 4) for d in (1, 3)]
    for dest in partners:
        pl.semaphore_signal(barrier, inc=1, device_id=dest, device_id_type=MESH)

    def wide(k):
        return pl.ds(pl.multiple_of(k * 768, 768), 768)

    def bo_chunk(k):
        return pltpu.make_async_copy(bo_ref.at[wide(k)], bo.at[c, wide(k)], bsem.at[k])

    def g_chunk(k):
        return pltpu.make_async_copy(
            g_ref.at[:, :, :, wide(k)], zp.at[k % 3, pl.ds(0, 3)], gsem.at[k % 3]
        )

    def bi_chunk(j):
        return pltpu.make_async_copy(
            bi_ref.at[j, :, :, wide(rep)], big.at[j, :, pl.ds(pl.multiple_of(m * 16, 16), 16)], tsem.at[j]
        )

    load_a = pltpu.make_async_copy(at_ref, ag.at[:, x, yl], lsem.at[0])
    load_a.start()
    for k in range(3):
        bo_chunk(k).start()
        g_chunk(k).start()
    for k in range(3, 8):
        bo_chunk(k).start()
    for j in range(parts):
        bi_chunk(j).start()

    def rows_half(h, n):
        return pl.ds(0, n) if h is None else pl.ds(h * (n // 2), n // 2)

    ga = Gather(lambda j, p, q, h: ag.at[j, q, p, rows_half(h, 128)], a_s, a_r, yl, x, over_owner)
    gb = Gather(
        lambda j, p, q, h: big.at[j, rows_half(h, 8), pl.ds(pl.multiple_of((p * 4 + q) * 16, 16), 16)],
        b_s, b_r, yl, x, over_owner,
    )
    gw = Gather(lambda j, p, q, h: wg.at[j, q * 2 + p, rows_half(h, 128)], w_s, w_r, yh, z, over_dp)
    go = Gather(lambda j, p, q, h: outg.at[j, q * 2 + p, rows_half(h, 256)], o_s, o_r, yh, z, over_dp)
    wp = zp
    rz = Reduce(zp, (z1, z2, z3, z4), (zs, zr, zps, zpr), yh, z, over_dp)
    rp = Reduce(pp, (p1, p2, p3, p4), (ps, pr, pps, ppr), yh, z, over_dp)
    rw = Reduce(wp, (w1, w2, w3, w4), (xs, xr, xps, xpr), yl, x, over_owner)

    load_a.wait()
    pl.semaphore_wait(barrier, len(partners))
    ga.first(0)
    send_bo = remote(bo_ref, bo.at[c], sib_s.at[0], sib_r.at[0], sibling)

    half = pl.ds(0, 384)
    acc[:, half] = jnp.zeros((768, 384), f32)

    def y_steps(low, high):
        @pl.loop(low, high)
        def _(k):
            bo_chunk(k).wait()
            g_chunk(k).wait()
            part = zp[k % 3, pl.ds(0, 3)].reshape(768, 768)
            acc[:, half] += jnp.dot(part, bo[c, wide(k), :], preferred_element_type=f32)

            @pl.when(k < 5)
            def _():
                g_chunk(k + 3).start()

    mine = pl.ds(pl.multiple_of(c * 384, 128), 384)
    other = pl.ds(pl.multiple_of(oc * 384, 128), 384)
    y_steps(0, 4)
    ga.second(0)
    ga.first(1)
    y_steps(4, 8)
    ym[:, mine] = acc[:, half].astype(bf16)
    send_y = remote(ym.at[:, mine], ym.at[:, mine], sib_s.at[1], sib_r.at[1], sibling)
    send_y.start()
    send_bo.start()
    ga.third(0)
    ga.second(1)
    ga.first(2)
    remote(ym.at[:, other], ym.at[:, other], sib_s.at[1], sib_r.at[1], sibling).wait_recv()

    def unit_dot(lhs, rhs):
        return jnp.dot(lhs.reshape(256, 768), rhs[...], preferred_element_type=f32).astype(bf16).reshape(2, 128, 768)

    def z_part(j):
        for d in (2, 1, 3, 0):
            t = (z + d) % 4
            zp[j, t] = unit_dot(ag[j, t], ym)
            if d == 2:
                rz.far(j)
        rz.near(j)

    def z_done(j):
        rows = pl.ds(pl.multiple_of(c * 384 + j * 128, 128), 128)
        zfull[rows, :] = rz.result(j).astype(bf16)

    ga.last(0)
    z_part(0)
    ga.third(1)
    ga.second(2)
    for j in range(parts):
        bi_chunk(j).wait()
    gb.first(0)
    ga.last(1)
    z_part(1)
    rz.merge(0)
    ga.third(2)
    gb.second(0)
    gb.first(1)
    ga.last(2)
    z_part(2)
    rz.merge(1)
    rz.swap(0)
    gb.third(0)
    gb.second(1)
    gb.first(2)
    rz.merge(2)
    z_done(0)
    rz.swap(1)
    z_done(1)
    gb.third(1)
    gb.second(2)
    rz.swap(2)
    z_done(2)

    def z_rows(core):
        return zfull.at[pl.ds(pl.multiple_of(core * 384, 128), 384)]

    send_z = remote(z_rows(c), z_rows(c), sib_s.at[2], sib_r.at[2], sibling)
    send_z.start()
    gb.third(2)
    for j in range(parts):
        ga.sent(j)
        rz.sent(j)
    remote(z_rows(oc), z_rows(oc), sib_s.at[2], sib_r.at[2], sibling).wait_recv()

    def p_part(j):
        for d in (2, 1, 3, 0):
            t = (z + d) % 4
            pp[j, t] = unit_dot(big[j, pl.ds(2 * t, 2)], zfull)
            if d == 2:
                rp.far(j)
        rp.near(j)

    def p_done(j):
        scale = ein_ref[j] * eout_ref[pl.ds(m, 1), :] + damping
        sc[j] = (rp.result(j) / scale).astype(bf16)

    nt = (((1,), (1,)), ((), ()))

    def w_part(j):
        for d in (2, 1, 3, 0):
            t = (x + d) % 4
            for h in range(2):
                rows = wide(h * 4 + t)
                part = lax.dot_general(sc[j, :, :384], bo[0, rows, :], nt, preferred_element_type=f32)
                part += lax.dot_general(sc[j, :, 384:], bo[1, rows, :], nt, preferred_element_type=f32)
                wp[j, t, h] = part.astype(bf16)
            if d == 2:
                rw.far(j)
        rw.near(j)

    def w_done(j):
        wg[j, z * 2 + yh] = rw.result(j).astype(bf16)
        gw.first(j)

    def out_part(j):
        @pl.loop(0, 4)
        def _(t):
            two = pl.ds(2 * t, 2)
            acc[...] += lax.dot_general(
                big[j, two].reshape(256, 768), wg[j, two].reshape(256, 768), (((0,), (0,)), ((), ())),
                preferred_element_type=f32,
            )

    gb.last(0)
    p_part(0)
    gb.last(1)
    rp.merge(0)
    p_part(1)
    rp.swap(0)
    rp.merge(1)
    gb.last(2)
    p_part(2)
    remote(bo_ref, bo.at[oc], sib_s.at[0], sib_r.at[0], sibling).wait_recv()
    p_done(0)
    w_part(0)
    rp.swap(1)
    rp.merge(2)
    rw.merge(0)
    p_done(1)
    w_part(1)
    rw.swap(0)
    rp.swap(2)
    rw.merge(1)
    w_done(0)
    p_done(2)
    w_part(2)
    acc[...] = jnp.zeros_like(acc)
    gw.second(0)
    rw.swap(1)
    rw.merge(2)
    gw.third(0)
    w_done(1)
    gw.last(0)
    out_part(0)
    gw.second(1)
    rw.swap(2)
    w_done(2)
    gw.third(1)
    gw.second(2)
    gw.last(1)
    out_part(1)
    gw.third(2)
    for j in range(parts):
        gb.sent(j)
        rp.sent(j)
        rw.sent(j)
    gw.last(2)
    out_part(2)

    send_f = remote(acc.at[:, other], frecv, sib_s.at[3], sib_r.at[3], sibling)
    send_f.start()
    remote(frecv, frecv, sib_s.at[3], sib_r.at[3], sibling).wait_recv()

    def o_rows(i):
        return pl.ds(i * 256, 256)

    def store(j, p, q):
        dst = o_ref.at[pl.ds(pl.multiple_of((p * 4 + q) * 768 + j * 256, 256), 256)]
        return pltpu.make_async_copy(outg.at[j, q * 2 + p], dst, osem.at[j, p, q])

    def stores(j, which):
        for dp, dq in which:
            store(j, (yh + dp) % 2, (z + dq) % 4).start()

    near = ((1, 0), (0, 3), (0, 1))
    nearer = ((1, 3), (1, 1))
    far = ((0, 2), (1, 2))
    for j in range(parts):
        outg[j, z * 2 + yh] = (acc[o_rows(j), mine] + frecv[o_rows(j), :]).astype(bf16)
        go.first(j)
        stores(j, ((0, 0),))
        if j >= 1:
            go.second(j - 1)
            stores(j - 1, near)
    go.third(0)
    stores(0, nearer)
    go.second(2)
    stores(2, near)
    go.last(0)
    stores(0, far)
    for j in (1, 2):
        go.third(j)
        stores(j, nearer)
        go.last(j)
        stores(j, far)
    for j in range(parts):
        gw.sent(j)
        go.sent(j)
    for cp in (send_bo, send_y, send_z, send_f):
        cp.wait_send()
    for j in range(parts):
        for p in range(2):
            for q in range(4):
                store(j, p, q).wait()


def shards(activations, out_grads, basis_in, basis_out, eig_in, eig_out):
    rep = lax.axis_index("dp")
    core = lax.axis_index("owner") % 2
    sub = (rep % 4) * 2 + rep // 4
    ein = lax.dynamic_slice(eig_in.reshape(8, 2, 3, 8, 16), (0, core, 0, sub, 0), (8, 1, 3, 1, 16))
    ein = ein.reshape(8, 3, 16).transpose(1, 0, 2).reshape(3, 128, 1)
    dma = pltpu.SemaphoreType.DMA
    v = pltpu.VMEM
    scratch = [
        v((3, 4, 2, 128, 768), bf16), v((768, 768), bf16), v((3, 4, 2, 128, 768), bf16), v((768, 768), bf16),
        v((3, 8, 128, 768), bf16), v((3, 4, 2, 128, 768), bf16), v((3, 128, 768), bf16),
        v((2, 6144, 384), bf16), v((3, 8, 128, 768), bf16), v((768, 768), f32), v((768, 384), f32),
        v((3, 8, 256, 384), bf16),
    ]
    scratch += [
        v((3, 2, 128, 768), bf16), v((3, 2, 2, 128, 768), bf16), v((3, 128, 768), bf16), v((3, 128, 768), bf16)
    ] * 3
    scratch += [dma((1,)), dma((3,)), dma((8,)), dma((3,)), dma((3, 2, 4))]
    scratch += [dma((3, 9))] * 8
    scratch += [dma((3, 6)), dma((3, 6)), dma((3,)), dma((3,))] * 3
    scratch += [dma((4,))] * 2
    hbm = pl.BlockSpec(memory_space=pl.ANY)
    vmem = pl.BlockSpec(memory_space=pltpu.VMEM)
    return pl.pallas_call(
        kernel,
        out_shape=jax.ShapeDtypeStruct((6144, 384), bf16),
        in_specs=[hbm, hbm, hbm, hbm, vmem, vmem],
        out_specs=hbm,
        scratch_shapes=scratch,
        compiler_params=pltpu.CompilerParams(
            collective_id=0, has_side_effects=True, vmem_limit_bytes=63 * 2**20
        ),
        name="precondition",
    )(
        activations.T.reshape(3, 128, 768), out_grads.reshape(3, 2, 128, 6144),
        basis_in.reshape(3, 8, 16, 6144), basis_out, ein, eig_out.reshape(8, 768),
    )


def solution(mesh):
    in_specs = (P("dp", "owner"), P("dp", None), P("owner", None), P(None, "owner"), P(), P())
    out_specs = P(None, "owner")
    return jax.shard_map(shards, mesh=mesh, in_specs=in_specs, out_specs=out_specs, check_vma=False)
```

```python
import jax
import jax.numpy as jnp
from jax import lax
from jax.experimental import pallas as pl
from jax.experimental.pallas import tpu as pltpu
from jax.sharding import PartitionSpec as P

damping = 0.1
bf16 = jnp.bfloat16
f32 = jnp.float32
MESH = pl.DeviceIdType.MESH
a_parts, p_parts, b_parts, o_parts = 6, 6, 3, 3
a_rows, p_rows, b_rows, o_rows = 384 // a_parts, 384 // p_parts, 384 // b_parts, 768 // o_parts
a_ways, b_ways, g_ways, o_ways = 'yyyyyy', 'yyy', 'yyyyyy', 'yxy'
order = (
    "A.first.0", "A.first.1", "Y.0", "Y.1", "A.f0.0", "A.f1.0", "A.first.2", "A.f2.0", "Y.2", "A.f0.1",
    "A.f1.1", "A.first.3", "A.f2.1", "Y.3", "Y.4", "A.f3.0", "A.f4.0", "A.f0.2", "Y.5", "A.f2.2", "A.f0.3",
    "Y.6", "A.f1.2", "A.first.4", "Y.7", "A.f3.1", "A.f4.1", "yout", "A.f2.3", "A.f0.4", "A.f1.3",
    "A.first.5", "Zc.0", "Z.go.0", "A.f3.2", "A.f4.2", "A.f0.5", "A.f3.3", "A.f4.3", "Z.m0.0", "Z.m1.0",
    "A.f1.4", "A.f2.4", "Zc.1", "Z.go.1", "Z.swap.0", "A.f3.4", "A.f4.4", "Z.m0.1", "Z.m1.1", "A.f1.5",
    "A.f2.5", "Zr.0", "Zc.2", "Z.go.2", "A.f3.5", "A.f4.5", "B.first.0", "Z.swap.1", "Zc.3", "Z.m0.2",
    "Z.m1.2", "Z.go.3", "Zc.4", "Zc.5", "B.f0.0", "Z.swap.2", "Zr.1", "Z.m0.3", "Z.m1.3", "Z.go.4", "B.f1.0",
    "B.first.1", "B.f2.0", "Zr.2", "Z.swap.3", "B.f3.0", "B.f4.0", "Z.m0.4", "Z.m1.4", "B.f0.1", "Z.go.5",
    "Zr.3", "B.f2.1", "Z.swap.4", "B.f1.1", "B.first.2", "Z.m0.5", "Z.m1.5", "Zr.4", "Z.swap.5", "B.f3.1",
    "B.f4.1", "B.f0.2", "Zr.5", "Pc.0", "B.f1.2", "B.f2.2", "P.go.0", "Pc.1", "Pc.2", "Pc.3", "P.m0.0",
    "P.m1.0", "P.go.1", "B.f3.2", "B.f4.2", "P.swap.0", "P.m0.1", "P.m1.1", "P.go.2", "Pc.4", "Pc.5", "Pr.0",
    "Wc.0", "W.go.0", "P.swap.1", "P.m0.2", "P.m1.2", "P.go.3", "W.m0.0", "W.m1.0", "Pr.1", "Wc.1", "W.go.1",
    "P.swap.2", "P.m0.3", "P.m1.3", "P.go.4", "W.swap.0", "W.m0.1", "W.m1.1", "Pr.2", "Wc.2", "P.m0.4",
    "P.m1.4", "P.go.5", "W.go.2", "P.swap.3", "Wr.0", "G.first.0", "W.swap.1", "P.swap.4", "W.m0.2", "W.m1.2",
    "Pr.3", "Wc.3", "P.m0.5", "P.m1.5", "G.f0.0", "W.go.3", "W.swap.2", "Wr.1", "G.first.1", "G.f1.0",
    "G.f2.0", "Pr.4", "Wc.4", "W.m0.3", "W.m1.3", "W.go.4", "P.swap.5", "Wr.2", "G.first.2", "G.f3.0",
    "G.f4.0", "G.f0.1", "G.f1.1", "G.f2.1", "W.swap.3", "Pr.5", "Wc.5", "W.m0.4", "W.m1.4", "G.f1.2",
    "G.f2.2", "G.f0.2", "W.go.5", "Oc.0", "Wr.3", "G.first.3", "G.f3.1", "G.f4.1", "W.swap.4", "W.m0.5",
    "W.m1.5", "G.f0.3", "G.f3.2", "G.f4.2", "Wr.4", "G.first.4", "G.f1.3", "G.f2.3", "Oc.1", "W.swap.5",
    "G.f3.3", "G.f4.3", "G.f0.4", "Oc.2", "Wr.5", "G.first.5", "G.f1.4", "G.f2.4", "Oc.3", "G.f0.5", "G.f3.4",
    "G.f4.4", "G.f1.5", "G.f2.5", "G.f3.5", "G.f4.5", "Oc.4", "Oc.5", "fsend", "osum.0", "O.first.0",
    "osum.1", "O.first.1", "osum.2", "O.first.2", "O.f0.0", "O.f1.0", "O.f2.0", "O.f0.1", "O.f1.1", "O.f0.2",
    "O.f1.2", "O.f2.2", "O.f3.0", "O.f4.0", "O.f2.1", "O.f3.2", "O.f4.2",
)


def device(yh, z, yl, x, c):
    return (yh * 4 + z, yl * 8 + x * 2 + c)


def remote(src, dst, s, r, dest):
    return pltpu.make_async_remote_copy(src, dst, s, r, device_id=dest, device_id_type=MESH)


class Gather:
    def __init__(self, part, ways, ssem, rsem, p, q, to):
        self.part, self.ways, self.ssem, self.rsem, self.p, self.q, self.to = part, ways, ssem, rsem, p, q, to

    def plan(self, j):
        p, q = self.p, self.q
        o, r, l, a = 1 - p, (q + 1) % 4, (q + 3) % 4, (q + 2) % 4
        if self.ways[j] == "y":
            return (
                ((p, q, None), (o, q), (o, q, None)),
                ((p, q, None), (p, r), (p, l, None)),
                ((p, q, None), (p, l), (p, r, None)),
                ((o, q, None), (p, r), (o, l, None)),
                ((o, q, None), (p, l), (o, r, None)),
                ((p, l, 0), (p, r), (p, a, 0)),
                ((p, r, 1), (p, l), (p, a, 1)),
                ((o, l, 0), (p, r), (o, a, 0)),
                ((o, r, 1), (p, l), (o, a, 1)),
            )
        return (
            ((p, q, None), (p, r), (p, l, None)),
            ((p, q, None), (p, l), (p, r, None)),
            ((p, l, 0), (p, r), (p, a, 0)),
            ((p, r, 1), (p, l), (p, a, 1)),
            ((p, q, None), (o, q), (o, q, None)),
            ((p, l, None), (o, q), (o, l, None)),
            ((p, r, None), (o, q), (o, r, None)),
            ((p, a, None), (o, q), (o, a, None)),
        )

    def copy(self, j, k):
        block, dest, _ = self.plan(j)[k]
        ref = self.part(j, *block)
        return remote(ref, ref, self.ssem.at[j, k], self.rsem.at[j, k], self.to(*dest))

    def start(self, j, *ks):
        for k in ks:
            self.copy(j, k).start()

    def got(self, j, *ks):
        for k in ks:
            _, dest, block = self.plan(j)[k]
            ref = self.part(j, *block)
            remote(ref, ref, self.ssem.at[j, k], self.rsem.at[j, k], self.to(*dest)).wait_recv()

    def step(self, what, j):
        if self.ways[j] == "y":
            waits, starts = {
                "first": ((), (0, 1, 2)),
                "f0": ((0,), (3, 4)),
                "f1": ((1,), (5,)),
                "f2": ((2,), (6,)),
                "f3": ((3,), (7,)),
                "f4": ((4,), (8,)),
                "last": ((5, 6, 7, 8), ()),
            }[what]
        else:
            waits, starts = {
                "first": ((), (0, 1, 4)),
                "f0": ((0,), (2, 5)),
                "f1": ((1,), (3, 6)),
                "f2": ((2, 3), (7,)),
                "last": ((4, 5, 6, 7), ()),
            }[what]
        self.got(j, *waits)
        self.start(j, *starts)

    def sent(self):
        for j in range(len(self.ways)):
            for k in range(len(self.plan(j))):
                self.copy(j, k).wait_send()


class Reduce:
    def __init__(self, n, src, bufs, sems, p, q, to):
        self.n, self.src, self.p, self.q, self.to = n, src, p, q, to
        self.mid, self.end, self.out, self.got = bufs
        self.ssem, self.rsem, self.psem, self.qsem = sems

    def copy(self, j, k):
        q = self.q
        r, l, a = (q + 1) % 4, (q + 3) % 4, (q + 2) % 4
        right, left = self.to(self.p, r), self.to(self.p, l)
        src, dst, dest = (
            (self.src.at[j, a, 0], self.mid.at[j, 0], right),
            (self.src.at[j, a, 1], self.mid.at[j, 1], left),
            (self.src.at[j, r, 1], self.end.at[j, 0, 1], right),
            (self.src.at[j, l, 0], self.end.at[j, 1, 0], left),
            (self.src.at[j, r, 0], self.end.at[j, 0, 0], right),
            (self.src.at[j, l, 1], self.end.at[j, 1, 1], left),
        )[k]
        return remote(src, dst, self.ssem.at[j, k], self.rsem.at[j, k], dest)

    def pair(self, j):
        return remote(
            self.out.at[j], self.got.at[j], self.psem.at[j], self.qsem.at[j], self.to(1 - self.p, self.q)
        )

    def total(self, j, h):
        return (
            self.src[j, self.q, h].astype(f32) + self.end[j, 0, h].astype(f32) + self.end[j, 1, h].astype(f32)
        )

    def step(self, what, j):
        if what == "go":
            for k in range(4):
                self.copy(j, k).start()
        elif what == "swap":
            for k in range(2, 6):
                self.copy(j, k).wait_recv()
            self.out[j] = self.total(j, 1 - self.p).astype(bf16)
            self.pair(j).start()
        else:
            h = 0 if what == "m0" else 1
            t = (self.q + 1 + 2 * h) % 4
            self.copy(j, h).wait_recv()
            self.src[j, t, h] = (self.src[j, t, h].astype(f32) + self.mid[j, h].astype(f32)).astype(bf16)
            self.copy(j, 4 + h).start()

    def result(self, j):
        self.pair(j).wait_recv()
        return self.total(j, self.p) + self.got[j].astype(f32)

    def sent(self):
        for j in range(self.n):
            for k in range(6):
                self.copy(j, k).wait_send()
            self.pair(j).wait_send()


def kernel(
    at_ref, g_ref, bi_ref, bo_ref, ein_ref, eout_ref, o_ref,
    ag, ym, zp, zfull, big, pp, sc, bo, wp, wg, acc, frecv, outg,
    z1, z2, z3, z4, p1, p2, p3, p4, w1, w2, w3, w4,
    lsem, gsem, bsem, tsem, osem,
    a_s, a_r, b_s, b_r, w_s, w_r, o_s, o_r,
    zs, zr, zps, zpr, ps, pr, pps, ppr, xs, xr, xps, xpr, sib_s, sib_r, zsib_s, zsib_r,
):
    rep = lax.axis_index("dp")
    own = lax.axis_index("owner")
    yh, z = rep // 4, rep % 4
    yl, x, c = own // 8, (own // 2) % 4, own % 2
    m = yl * 4 + x
    oc = 1 - c

    sibling = device(yh, z, yl, x, oc)
    over_owner = lambda p, q: device(yh, z, p, q, c)
    over_dp = lambda p, q: device(p, q, yl, x, c)

    barrier = pltpu.get_barrier_semaphore()
    partners = [sibling, over_dp(1 - yh, z), over_owner(1 - yl, x)]
    partners += [over_owner(yl, (x + d) % 4) for d in (1, 3)]
    partners += [over_dp(yh, (z + d) % 4) for d in (1, 3)]
    for dest in partners:
        pl.semaphore_signal(barrier, inc=1, device_id=dest, device_id_type=MESH)

    def at(start, size, step):
        return pl.ds(pl.multiple_of(start, step), size)

    def wide(k):
        return at(k * 768, 768, 768)

    def halves(h, n):
        return pl.ds(0, n) if h is None else pl.ds(h * (n // 2), n // 2)

    def bo_chunk(k):
        return pltpu.make_async_copy(bo_ref.at[wide(k)], bo.at[c, wide(k)], bsem.at[k])

    def g_chunk(k):
        b = k % 4
        return pltpu.make_async_copy(g_ref.at[:, :, :, wide(k)], wg.at[:, pl.ds(2 * b, 2)], gsem.at[b])

    def bi_chunk(j):
        return pltpu.make_async_copy(
            bi_ref.at[j, :, :, wide(rep)], big.at[j, :, at(m * 16, 16, 16)], tsem.at[j]
        )

    load_a = pltpu.make_async_copy(at_ref, ag.at[:, x, yl], lsem.at[0])
    load_a.start()
    for k in range(4):
        bo_chunk(k).start()
        g_chunk(k).start()
    for k in range(4, 8):
        bo_chunk(k).start()
    for j in range(b_parts):
        bi_chunk(j).start()

    ga = Gather(lambda j, p, q, h: ag.at[j, q, p, halves(h, a_rows)], a_ways, a_s, a_r, yl, x, over_owner)
    gb = Gather(
        lambda j, p, q, h: big.at[j, halves(h, 8), at((p * 4 + q) * 16, 16, 16)],
        b_ways, b_s, b_r, yl, x, over_owner,
    )
    gw = Gather(lambda j, p, q, h: wg.at[j, q * 2 + p, halves(h, p_rows)], g_ways, w_s, w_r, yh, z, over_dp)
    go = Gather(lambda j, p, q, h: outg.at[j, q * 2 + p, halves(h, o_rows)], o_ways, o_s, o_r, yh, z, over_dp)
    rz = Reduce(a_parts, zp, (z1, z2, z3, z4), (zs, zr, zps, zpr), yh, z, over_dp)
    rp = Reduce(p_parts, pp, (p1, p2, p3, p4), (ps, pr, pps, ppr), yh, z, over_dp)
    rw = Reduce(p_parts, wp, (w1, w2, w3, w4), (xs, xr, xps, xpr), yl, x, over_owner)

    half = pl.ds(0, 384)
    mine, other = at(c * 384, 384, 128), at(oc * 384, 384, 128)
    send_bo = remote(bo_ref, bo.at[c], sib_s.at[0], sib_r.at[0], sibling)
    send_y = remote(ym.at[:, mine], ym.at[:, mine], sib_s.at[1], sib_r.at[1], sibling)
    send_f = remote(acc.at[:, other], frecv, sib_s.at[2], sib_r.at[2], sibling)
    group = p_parts // b_parts
    nt = (((1,), (1,)), ((), ()))
    tn = (((0,), (0,)), ((), ()))

    def y_step(k):
        bo_chunk(k).wait()
        g_chunk(k).wait()
        b = k % 4
        lhs = wg[:, pl.ds(2 * b, 2)].reshape(768, 768)
        part = jnp.dot(lhs, bo[c, wide(k), :], preferred_element_type=f32)
        acc[:, half] = part if k == 0 else acc[:, half] + part
        if k + 4 < 8:
            g_chunk(k + 4).start()

    def y_out():
        ym[:, mine] = acc[:, half].astype(bf16)
        send_y.start()
        send_bo.start()

    def z_part(j):
        if j == 0:
            remote(ym.at[:, other], ym.at[:, other], sib_s.at[1], sib_r.at[1], sibling).wait_recv()
        ga.step("last", j)

        @pl.loop(0, 2)
        def _(t):
            two = pl.ds(2 * t, 2)
            part = jnp.dot(ag[j, two].reshape(4 * a_rows, 768), ym[...], preferred_element_type=f32)
            zp[j, two] = part.astype(bf16).reshape(2, 2, a_rows, 768)

    def z_copy(j, core):
        ref = zfull.at[at(core * 384 + j * a_rows, a_rows, a_rows)]
        return remote(ref, ref, zsib_s.at[j], zsib_r.at[j], sibling)

    def z_done(j):
        zfull[at(c * 384 + j * a_rows, a_rows, a_rows), :] = rz.result(j).astype(bf16)
        z_copy(j, c).start()

    def p_part(j):
        if j == 0:
            for i in range(a_parts):
                z_copy(i, oc).wait_recv()
        if j % group == 0:
            gb.step("last", j // group)
        rows = pl.ds((j % group) * p_rows, p_rows)

        @pl.loop(0, 2)
        def _(t):
            lhs = big[j // group, pl.ds(4 * t, 4), rows, :].reshape(4 * p_rows, 768)
            part = jnp.dot(lhs, zfull[...], preferred_element_type=f32)
            pp[j, pl.ds(2 * t, 2)] = part.astype(bf16).reshape(2, 2, p_rows, 768)

    def p_done(j):
        scale = ein_ref[j] * eout_ref[pl.ds(m, 1), :] + damping
        sc[j] = (rp.result(j) / scale).astype(bf16)

    def w_part(j):
        if j == 0:
            remote(bo_ref, bo.at[oc], sib_s.at[0], sib_r.at[0], sibling).wait_recv()

        @pl.loop(0, 8)
        def _(t):
            rows = wide((t % 2) * 4 + t // 2)
            part = lax.dot_general(sc[j, :, :384], bo[0, rows, :], nt, preferred_element_type=f32)
            part += lax.dot_general(sc[j, :, 384:], bo[1, rows, :], nt, preferred_element_type=f32)
            wp[j, t // 2, t % 2] = part.astype(bf16)

    def w_done(j):
        wg[j, z * 2 + yh] = rw.result(j).astype(bf16)

    def out_part(j):
        gw.step("last", j)
        rows = pl.ds((j % group) * p_rows, p_rows)
        lhs = big[j // group, :, rows, :].reshape(8 * p_rows, 768)
        part = lax.dot_general(lhs, wg[j].reshape(8 * p_rows, 768), tn, preferred_element_type=f32)
        acc[...] = part if j == 0 else acc[...] + part

    def store(j, p, q):
        dst = o_ref.at[at((p * 4 + q) * 768 + j * o_rows, o_rows, o_rows)]
        return pltpu.make_async_copy(outg.at[j, q * 2 + p], dst, osem.at[j, p, q])

    def out_sum(j):
        if j == 0:
            remote(frecv, frecv, sib_s.at[2], sib_r.at[2], sibling).wait_recv()
        rows = pl.ds(j * o_rows, o_rows)
        outg[j, z * 2 + yh] = (acc[rows, mine] + frecv[rows, :]).astype(bf16)

    others = {
        "Zc": z_part, "Zr": z_done, "Pc": p_part, "Pr": p_done, "Wc": w_part, "Wr": w_done, "Oc": out_part,
        "osum": out_sum, "Y": y_step,
    }
    movers = {"A": ga, "B": gb, "G": gw, "O": go, "Z": rz, "P": rp, "W": rw}

    load_a.wait()
    pl.semaphore_wait(barrier, len(partners))
    for step in order:
        name = step.split(".")
        if name[0] in others:
            others[name[0]](int(name[1]))
        elif name[0] in movers:
            if name[0] == "B" and name[1] == "first":
                bi_chunk(int(name[2])).wait()
            movers[name[0]].step(name[1], int(name[2]))
        elif step == "yout":
            y_out()
        else:
            send_f.start()

    for dp, dq in ((0, 0), (1, 0), (0, 1), (0, 3), (1, 1), (1, 3), (0, 2), (1, 2)):
        if (dp, dq) == (1, 0):
            for j in range(o_parts):
                go.step("last", j)
        for j in range(o_parts):
            store(j, (yh + dp) % 2, (z + dq) % 4).start()
    for mover in (ga, gb, gw, go, rz, rp, rw):
        mover.sent()
    for cp in (send_bo, send_y, send_f):
        cp.wait_send()
    for j in range(a_parts):
        z_copy(j, c).wait_send()
    for j in range(o_parts):
        for p in range(2):
            for q in range(4):
                store(j, p, q).wait()


def shards(activations, out_grads, basis_in, basis_out, eig_in, eig_out):
    rep = lax.axis_index("dp")
    core = lax.axis_index("owner") % 2
    sub = (rep % 4) * 2 + rep // 4
    ein = lax.dynamic_slice(eig_in.reshape(8, 2, 3, 8, 16), (0, core, 0, sub, 0), (8, 1, 3, 1, 16))
    ein = ein.reshape(8, 3, 16).transpose(1, 0, 2).reshape(p_parts, p_rows, 1)
    dma = pltpu.SemaphoreType.DMA
    v = pltpu.VMEM
    scratch = [
        v((a_parts, 4, 2, a_rows, 768), bf16), v((768, 768), bf16), v((a_parts, 4, 2, a_rows, 768), bf16),
        v((768, 768), bf16), v((b_parts, 8, b_rows, 768), bf16), v((p_parts, 4, 2, p_rows, 768), bf16),
        v((p_parts, p_rows, 768), bf16), v((2, 6144, 384), bf16), v((p_parts, 4, 2, p_rows, 768), bf16),
        v((p_parts, 8, p_rows, 768), bf16), v((768, 768), f32), v((768, 384), f32),
        v((o_parts, 8, o_rows, 384), bf16),
    ]
    for n, rows in ((a_parts, a_rows), (p_parts, p_rows), (p_parts, p_rows)):
        scratch += [
            v((n, 2, rows, 768), bf16), v((n, 2, 2, rows, 768), bf16), v((n, rows, 768), bf16),
            v((n, rows, 768), bf16),
        ]
    scratch += [dma((1,)), dma((4,)), dma((8,)), dma((b_parts,)), dma((o_parts, 2, 4))]
    for n in (a_parts, b_parts, p_parts, o_parts):
        scratch += [dma((n, 9))] * 2
    for n in (a_parts, p_parts, p_parts):
        scratch += [dma((n, 6))] * 2 + [dma((n,))] * 2
    scratch += [dma((3,))] * 2 + [dma((a_parts,))] * 2
    hbm = pl.BlockSpec(memory_space=pl.ANY)
    vmem = pl.BlockSpec(memory_space=pltpu.VMEM)
    return pl.pallas_call(
        kernel,
        out_shape=jax.ShapeDtypeStruct((6144, 384), bf16),
        in_specs=[hbm, hbm, hbm, hbm, vmem, vmem],
        out_specs=hbm,
        scratch_shapes=scratch,
        compiler_params=pltpu.CompilerParams(
            collective_id=0, has_side_effects=True, vmem_limit_bytes=64 * 2**20
        ),
        name="precondition",
    )(
        activations.T.reshape(a_parts, a_rows, 768), out_grads.reshape(p_parts, 2, p_rows, 6144),
        basis_in.reshape(b_parts, 8, 16, 6144), basis_out, ein, eig_out.reshape(8, 768),
    )


def solution(mesh):
    in_specs = (P("dp", "owner"), P("dp", None), P("owner", None), P(None, "owner"), P(), P())
    out_specs = P(None, "owner")
    return jax.shard_map(shards, mesh=mesh, in_specs=in_specs, out_specs=out_specs, check_vma=False)
```

```python
import jax
import jax.numpy as jnp
from jax import lax
from jax.experimental import pallas as pl
from jax.experimental.pallas import tpu as pltpu
from jax.sharding import PartitionSpec as P

damping = 0.1
bf16 = jnp.bfloat16
f32 = jnp.float32
MESH = pl.DeviceIdType.MESH
a_parts, p_parts, b_parts, o_parts = 6, 6, 3, 3
a_rows, p_rows, b_rows, o_rows = 384 // a_parts, 384 // p_parts, 384 // b_parts, 768 // o_parts
a_ways, b_ways, g_ways, o_ways = 'yxyyxy', 'yyy', 'yyyyyy', 'yxy'
steps = (
    "A.first", "Y", "A.f0", "A.f1", "A.f2", "A.f3", "A.f4", "yout", "T", "Zc", "Z.go", "Z.m0", "Z.m1", "Z.swap",
    "Zr", "B.first", "B.f0", "B.f1", "B.f2", "B.f3", "B.f4", "Pc", "P.go", "P.m0", "P.m1", "P.swap", "Pr", "Wc",
    "W.go", "W.m0", "W.m1", "W.swap", "Wr", "G.first", "G.f0", "G.f1", "G.f2", "G.f3", "G.f4", "Oc", "fsend",
    "osum", "O.first", "O.f0", "O.f1", "O.f2", "O.f3", "O.f4",
)
order = (
    0, 1, 16, 17, 18, 32, 48, 2, 64, 19, 20, 33, 49, 3, 21, 22, 80, 96, 34, 23, 112, 66, 50, 4, 128, 65, 129,
    130, 131, 51, 67, 35, 5, 144, 160, 82, 98, 145, 176, 192, 161, 36, 52, 37, 83, 99, 208, 53, 69, 177, 193,
    146, 68, 162, 224, 85, 101, 240, 209, 147, 148, 178, 194, 163, 149, 256, 210, 272, 241, 288, 225, 179, 195,
    164, 226, 304, 320, 211, 257, 180, 196, 165, 289, 227, 273, 242, 212, 181, 197, 258, 305, 321, 213, 228,
    229, 274, 290, 336, 352, 337, 306, 322, 368, 384, 353, 338, 339, 400, 340, 341, 369, 385, 354, 416, 432,
    448, 401, 370, 386, 355, 464, 480, 417, 433, 371, 387, 356, 449, 402, 496, 403, 465, 481, 418, 434, 372,
    388, 357, 450, 512, 528, 497, 419, 435, 466, 482, 544, 451, 404, 373, 389, 513, 529, 498, 420, 436, 560,
    576, 467, 483, 545, 592, 608, 452, 514, 530, 405, 561, 577, 499, 546, 468, 484, 593, 609, 421, 437, 562,
    578, 453, 515, 531, 500, 624, 594, 610, 625, 469, 485, 547, 563, 579, 516, 532, 626, 501, 595, 611, 548,
    564, 580, 517, 533, 627, 596, 612, 549, 565, 581, 628, 597, 613, 629, 640, 656, 672, 657, 673, 658, 674,
    688, 704, 720, 689, 705, 690, 706, 722, 736, 752, 721, 738, 754,
)


def device(yh, z, yl, x, c):
    return (yh * 4 + z, yl * 8 + x * 2 + c)


def remote(src, dst, s, r, dest):
    return pltpu.make_async_remote_copy(src, dst, s, r, device_id=dest, device_id_type=MESH)


class Gather:
    def __init__(self, part, ways, ssem, rsem, p, q, to):
        self.part, self.ways, self.ssem, self.rsem, self.p, self.q, self.to = part, ways, ssem, rsem, p, q, to

    def plan(self, j):
        p, q = self.p, self.q
        o, r, l, a = 1 - p, (q + 1) % 4, (q + 3) % 4, (q + 2) % 4
        if self.ways[j] == "y":
            return (
                ((p, q, None), (o, q), (o, q, None)),
                ((p, q, None), (p, r), (p, l, None)),
                ((p, q, None), (p, l), (p, r, None)),
                ((o, q, None), (p, r), (o, l, None)),
                ((o, q, None), (p, l), (o, r, None)),
                ((p, l, 0), (p, r), (p, a, 0)),
                ((p, r, 1), (p, l), (p, a, 1)),
                ((o, l, 0), (p, r), (o, a, 0)),
                ((o, r, 1), (p, l), (o, a, 1)),
            )
        return (
            ((p, q, None), (p, r), (p, l, None)),
            ((p, q, None), (p, l), (p, r, None)),
            ((p, l, 0), (p, r), (p, a, 0)),
            ((p, r, 1), (p, l), (p, a, 1)),
            ((p, q, None), (o, q), (o, q, None)),
            ((p, l, None), (o, q), (o, l, None)),
            ((p, r, None), (o, q), (o, r, None)),
            ((p, a, None), (o, q), (o, a, None)),
        )

    def copy(self, j, k):
        block, dest, _ = self.plan(j)[k]
        ref = self.part(j, *block)
        return remote(ref, ref, self.ssem.at[j, k], self.rsem.at[j, k], self.to(*dest))

    def start(self, j, *ks):
        for k in ks:
            self.copy(j, k).start()

    def got(self, j, *ks):
        for k in ks:
            _, dest, block = self.plan(j)[k]
            ref = self.part(j, *block)
            remote(ref, ref, self.ssem.at[j, k], self.rsem.at[j, k], self.to(*dest)).wait_recv()

    def step(self, what, j):
        if self.ways[j] == "y":
            waits, starts = {
                "first": ((), (0, 1, 2)),
                "f0": ((0,), (3, 4)),
                "f1": ((1,), (5,)),
                "f2": ((2,), (6,)),
                "f3": ((3,), (7,)),
                "f4": ((4,), (8,)),
                "last": ((5, 6, 7, 8), ()),
            }[what]
        else:
            waits, starts = {
                "first": ((), (0, 1, 4)),
                "f0": ((0,), (2, 5)),
                "f1": ((1,), (3, 6)),
                "f2": ((2, 3), (7,)),
                "last": ((4, 5, 6, 7), ()),
            }[what]
        self.got(j, *waits)
        self.start(j, *starts)

    def sent(self):
        for j in range(len(self.ways)):
            for k in range(len(self.plan(j))):
                self.copy(j, k).wait_send()


class Reduce:
    def __init__(self, src, bufs, sems, p, q, to):
        self.src, self.p, self.q, self.to = src, p, q, to
        self.mid, self.end, self.out, self.got = bufs
        self.ssem, self.rsem, self.psem, self.qsem = sems

    def copy(self, j, k):
        q = self.q
        r, l, a = (q + 1) % 4, (q + 3) % 4, (q + 2) % 4
        right, left = self.to(self.p, r), self.to(self.p, l)
        src, dst, dest = (
            (self.src.at[j, a, 0], self.mid.at[j, 0], right),
            (self.src.at[j, a, 1], self.mid.at[j, 1], left),
            (self.src.at[j, r, 1], self.end.at[j, 0, 1], right),
            (self.src.at[j, l, 0], self.end.at[j, 1, 0], left),
            (self.src.at[j, r, 0], self.end.at[j, 0, 0], right),
            (self.src.at[j, l, 1], self.end.at[j, 1, 1], left),
        )[k]
        return remote(src, dst, self.ssem.at[j, k], self.rsem.at[j, k], dest)

    def pair(self, j):
        return remote(
            self.out.at[j], self.got.at[j], self.psem.at[j], self.qsem.at[j], self.to(1 - self.p, self.q)
        )

    def total(self, j, h):
        return (
            self.src[j, self.q, h].astype(f32) + self.end[j, 0, h].astype(f32) + self.end[j, 1, h].astype(f32)
        )

    def step(self, what, j):
        if what == "go":
            for k in range(4):
                self.copy(j, k).start()
        elif what == "swap":
            for k in range(2, 6):
                self.copy(j, k).wait_recv()
            self.out[j] = self.total(j, 1 - self.p).astype(bf16)
            self.pair(j).start()
        else:
            h = 0 if what == "m0" else 1
            t = (self.q + 1 + 2 * h) % 4
            self.copy(j, h).wait_recv()
            self.src[j, t, h] = self.src[j, t, h] + self.mid[j, h]
            self.copy(j, 4 + h).start()

    def result(self, j):
        self.pair(j).wait_recv()
        return self.total(j, self.p) + self.got[j].astype(f32)

    def sent(self, j):
        for k in range(6):
            self.copy(j, k).wait_send()
        self.pair(j).wait_send()


def kernel(
    a_ref, g_ref, bi_ref, bo_ref, ein_ref, eout_ref, o_ref,
    am, ag, ym, zp, zfull, big, pp, sc, bo, bot, wg, acc, frecv, outg, es,
    z1, z2, z3, z4, p1, p2, p3, p4, w1, w2, w3, w4,
    lsem, gsem, bsem, tsem, osem,
    a_s, a_r, b_s, b_r, w_s, w_r, o_s, o_r,
    zs, zr, zps, zpr, ps, pr, pps, ppr, xs, xr, xps, xpr, sib_s, sib_r, zsib_s, zsib_r,
):
    rep = lax.axis_index("dp")
    own = lax.axis_index("owner")
    yh, z = rep // 4, rep % 4
    yl, x, c = own // 8, (own // 2) % 4, own % 2
    m = yl * 4 + x
    oc = 1 - c

    sibling = device(yh, z, yl, x, oc)
    over_owner = lambda p, q: device(yh, z, p, q, c)
    over_dp = lambda p, q: device(p, q, yl, x, c)

    barrier = pltpu.get_barrier_semaphore()
    partners = [sibling, over_dp(1 - yh, z), over_owner(1 - yl, x)]
    partners += [over_owner(yl, (x + d) % 4) for d in (1, 3)]
    partners += [over_dp(yh, (z + d) % 4) for d in (1, 3)]
    for dest in partners:
        pl.semaphore_signal(barrier, inc=1, device_id=dest, device_id_type=MESH)

    def at(start, size, step):
        return pl.ds(pl.multiple_of(start, step), size)

    def wide(k):
        return at(k * 768, 768, 768)

    def halves(h, n):
        return pl.ds(0, n) if h is None else pl.ds(h * (n // 2), n // 2)

    def bo_chunk(k):
        return pltpu.make_async_copy(bo_ref.at[wide(k)], bo.at[wide(k)], bsem.at[k])

    def g_chunk(k):
        b = k % 4
        return pltpu.make_async_copy(g_ref.at[:, :, :, wide(k)], wg.at[:, pl.ds(2 * b, 2)], gsem.at[b])

    def bi_chunk(j):
        return pltpu.make_async_copy(
            bi_ref.at[j, :, :, wide(rep)], big.at[:, at(j * 128 + m * 16, 16, 16)], tsem.at[j]
        )

    load_a = pltpu.make_async_copy(a_ref, am, lsem.at[0])
    load_a.start()
    for k in range(4):
        bo_chunk(k).start()
        g_chunk(k).start()
    for k in range(4, 8):
        bo_chunk(k).start()
    for j in range(b_parts):
        bi_chunk(j).start()

    ga = Gather(lambda j, p, q, h: ag.at[j, q, p, halves(h, a_rows)], a_ways, a_s, a_r, yl, x, over_owner)
    gb = Gather(
        lambda j, p, q, h: big.at[halves(h, 8), at(j * 128 + (p * 4 + q) * 16, 16, 16)],
        b_ways, b_s, b_r, yl, x, over_owner,
    )
    gw = Gather(lambda j, p, q, h: wg.at[j, q * 2 + p, halves(h, p_rows)], g_ways, w_s, w_r, yh, z, over_dp)
    go = Gather(lambda j, p, q, h: outg.at[j, q * 2 + p, halves(h, o_rows)], o_ways, o_s, o_r, yh, z, over_dp)
    rz = Reduce(zp, (z1, z2, z3, z4), (zs, zr, zps, zpr), yh, z, over_dp)
    rp = Reduce(pp, (p1, p2, p3, p4), (ps, pr, pps, ppr), yh, z, over_dp)
    rw = Reduce(pp, (w1, w2, w3, w4), (xs, xr, xps, xpr), yl, x, over_owner)

    half = pl.ds(0, 384)
    mine, other = at(c * 384, 384, 128), at(oc * 384, 384, 128)

    def bot_copy(core):
        ref = bot.at[at(core * 384, 384, 128)]
        return remote(ref, ref, sib_s.at[0], sib_r.at[0], sibling)

    send_y = remote(ym.at[:, mine], ym.at[:, mine], sib_s.at[1], sib_r.at[1], sibling)
    send_f = remote(acc.at[:, other], frecv, sib_s.at[2], sib_r.at[2], sibling)
    tn = (((0,), (0,)), ((), ()))

    lane = lax.broadcasted_iota(jnp.int32, (16, 128), 1)
    place = lax.broadcasted_iota(jnp.int32, (16, 128), 0) + (z * 2 + yh) * 16

    def eigen(_):
        @pl.loop(0, 24)
        def _(i):
            row = ein_ref[pl.ds((2 * (i % 8) + c) * 3 + i // 8, 1), :]
            column = jnp.sum(jnp.where(lane == place, row, 0.0), axis=1, keepdims=True)
            es[at(i * 16, 16, 16), :] = jnp.broadcast_to(column, (16, 128))

    def y_step(k):
        bo_chunk(k).wait()
        g_chunk(k).wait()
        b = k % 4
        lhs = wg[:, pl.ds(2 * b, 2)].reshape(768, 768)
        part = jnp.dot(lhs, bo[wide(k), :], preferred_element_type=f32)
        acc[:, half] = part if k == 0 else acc[:, half] + part
        if k + 4 < 8:
            g_chunk(k + 4).start()

    def y_out(_):
        ym[:, mine] = acc[:, half].astype(bf16)
        send_y.start()

    def turn(k):
        rows = pl.ds(k * 1536, 1536)
        bot[mine, rows] = bo[rows, :].T
        if k == 0:
            eigen(k)
        if k == 3:
            bot_copy(c).start()

    def z_part(j):
        if j == 0:
            remote(ym.at[:, other], ym.at[:, other], sib_s.at[1], sib_r.at[1], sibling).wait_recv()
        ga.step("last", j)

        @pl.loop(0, 2)
        def _(t):
            two = pl.ds(2 * t, 2)
            part = jnp.dot(ag[j, two].reshape(4 * a_rows, 768), ym[...], preferred_element_type=f32)
            zp[j, two] = part.astype(bf16).reshape(2, 2, a_rows, 768)

    def z_copy(j, core):
        ref = zfull.at[at(core * 384 + j * a_rows, a_rows, a_rows)]
        return remote(ref, ref, zsib_s.at[j], zsib_r.at[j], sibling)

    def z_done(j):
        zfull[at(c * 384 + j * a_rows, a_rows, a_rows), :] = rz.result(j).astype(bf16)
        z_copy(j, c).start()

    bi_seen = [0]

    def p_part(j):
        if j == 0:
            for i in range(a_parts):
                z_copy(i, oc).wait_recv()
        while bi_seen[0] * b_rows < (j + 1) * p_rows:
            gb.step("last", bi_seen[0])
            bi_seen[0] += 1
        rows = pl.ds(j * p_rows, p_rows)

        @pl.loop(0, 2)
        def _(t):
            lhs = big[pl.ds(4 * t, 4), rows, :].reshape(4 * p_rows, 768)
            part = jnp.dot(lhs, zfull[...], preferred_element_type=f32)
            pp[j, pl.ds(2 * t, 2)] = part.astype(bf16).reshape(2, 2, p_rows, 768)

    def p_done(j):
        total = rp.result(j)
        for b in range(6):
            cols = slice(b * 128, (b + 1) * 128)
            scale = es[pl.ds(j * p_rows, p_rows), :] * eout_ref[pl.ds(m * 6 + b, 1), :] + damping
            sc[j, :, cols] = (total[:, cols] / scale).astype(bf16)

    def w_part(j):
        if j == 0:
            bot_copy(oc).wait_recv()
        rp.sent(j)

        @pl.loop(0, 8)
        def _(t):
            cols = wide((t % 2) * 4 + t // 2)
            pp[j, t // 2, t % 2] = jnp.dot(sc[j], bot[:, cols], preferred_element_type=f32).astype(bf16)

    def w_done(j):
        wg[j, z * 2 + yh] = rw.result(j).astype(bf16)

    def out_part(j):
        gw.step("last", j)
        lhs = big[:, pl.ds(j * p_rows, p_rows), :].reshape(8 * p_rows, 768)
        part = lax.dot_general(lhs, wg[j].reshape(8 * p_rows, 768), tn, preferred_element_type=f32)
        acc[...] = part if j == 0 else acc[...] + part

    def store(j, p, q):
        dst = o_ref.at[at((p * 4 + q) * 768 + j * o_rows, o_rows, o_rows)]
        return pltpu.make_async_copy(outg.at[j, q * 2 + p], dst, osem.at[j, p, q])

    def out_sum(j):
        if j == 0:
            remote(frecv, frecv, sib_s.at[2], sib_r.at[2], sibling).wait_recv()
        rows = pl.ds(j * o_rows, o_rows)
        outg[j, z * 2 + yh] = (acc[rows, mine] + frecv[rows, :]).astype(bf16)

    def f_out(_):
        send_f.start()

    others = {
        "Zc": z_part, "Zr": z_done, "Pc": p_part, "Pr": p_done, "Wc": w_part, "Wr": w_done, "Oc": out_part,
        "osum": out_sum, "T": turn, "Y": y_step, "yout": y_out, "fsend": f_out,
    }
    movers = {"A": ga, "B": gb, "G": gw, "O": go, "Z": rz, "P": rp, "W": rw}

    load_a.wait()
    for t in range(3):
        per = 128 // a_rows
        ag[pl.ds(t * per, per), x, yl] = am[:, t * 128 : (t + 1) * 128].T.reshape(per, a_rows, 768)
    pl.semaphore_wait(barrier, len(partners))
    for step in order:
        name, j = steps[step // 16].split("."), step % 16
        if len(name) == 1:
            others[name[0]](j)
        else:
            if name == ["B", "first"]:
                bi_chunk(j).wait()
            movers[name[0]].step(name[1], j)

    for dp, dq in ((0, 0), (1, 0), (0, 1), (0, 3), (1, 1), (1, 3), (0, 2), (1, 2)):
        if (dp, dq) == (1, 0):
            for j in range(o_parts):
                go.step("last", j)
        for j in range(o_parts):
            store(j, (yh + dp) % 2, (z + dq) % 4).start()
    for gather in (ga, gb, gw, go):
        gather.sent()
    for j in range(a_parts):
        rz.sent(j)
    for j in range(p_parts):
        rw.sent(j)
    for cp in (bot_copy(c), send_y, send_f):
        cp.wait_send()
    for j in range(a_parts):
        z_copy(j, c).wait_send()
    for j in range(o_parts):
        for p in range(2):
            for q in range(4):
                store(j, p, q).wait()


def shards(activations, out_grads, basis_in, basis_out, eig_in, eig_out):
    dma = pltpu.SemaphoreType.DMA
    v = pltpu.VMEM
    scratch = [
        v((768, 384), bf16), v((a_parts, 4, 2, a_rows, 768), bf16), v((768, 768), bf16),
        v((a_parts, 4, 2, a_rows, 768), bf16), v((768, 768), bf16), v((8, 384, 768), bf16),
        v((p_parts, 4, 2, p_rows, 768), bf16), v((p_parts, p_rows, 768), bf16), v((6144, 384), bf16),
        v((768, 6144), bf16), v((p_parts, 8, p_rows, 768), bf16), v((768, 768), f32), v((768, 384), f32),
        v((o_parts, 8, o_rows, 384), bf16), v((384, 128), f32),
    ]
    for n, rows in ((a_parts, a_rows), (p_parts, p_rows), (p_parts, p_rows)):
        scratch += [
            v((n, 2, rows, 768), bf16), v((n, 2, 2, rows, 768), bf16), v((n, rows, 768), bf16),
            v((n, rows, 768), bf16),
        ]
    scratch += [dma((1,)), dma((4,)), dma((8,)), dma((b_parts,)), dma((o_parts, 2, 4))]
    for n in (a_parts, b_parts, p_parts, o_parts):
        scratch += [dma((n, 9))] * 2
    for n in (a_parts, p_parts, p_parts):
        scratch += [dma((n, 6))] * 2 + [dma((n,))] * 2
    scratch += [dma((3,))] * 2 + [dma((a_parts,))] * 2
    hbm = pl.BlockSpec(memory_space=pl.ANY)
    vmem = pl.BlockSpec(memory_space=pltpu.VMEM)
    return pl.pallas_call(
        kernel,
        out_shape=jax.ShapeDtypeStruct((6144, 384), bf16),
        in_specs=[hbm, hbm, hbm, hbm, vmem, vmem],
        out_specs=hbm,
        scratch_shapes=scratch,
        compiler_params=pltpu.CompilerParams(
            collective_id=0, has_side_effects=True, vmem_limit_bytes=64 * 2**20
        ),
        name="precondition",
    )(
        activations, out_grads.reshape(p_parts, 2, p_rows, 6144), basis_in.reshape(b_parts, 8, 16, 6144), basis_out,
        eig_in.reshape(48, 128), eig_out.reshape(48, 128),
    )


def solution(mesh):
    in_specs = (P("dp", "owner"), P("dp", None), P("owner", None), P(None, "owner"), P(), P())
    out_specs = P(None, "owner")
    return jax.shard_map(shards, mesh=mesh, in_specs=in_specs, out_specs=out_specs, check_vma=False)
```

```python
import jax
import jax.numpy as jnp
from jax import lax
from jax.experimental import pallas as pl
from jax.experimental.pallas import tpu as pltpu
from jax.sharding import PartitionSpec as P

damping = 0.1
bf16 = jnp.bfloat16
f32 = jnp.float32
MESH = pl.DeviceIdType.MESH
a_parts, p_parts, b_parts, o_parts = 6, 6, 3, 6
a_rows, p_rows, b_rows, o_rows = 384 // a_parts, 384 // p_parts, 384 // b_parts, 768 // o_parts
a_ways, b_ways, g_ways, o_ways = 'yxyyxy', 'yyy', 'rrrrrr', 'yxyyxy'
steps = (
    "Y", "bar", "A.first", "A.f0", "A.f2", "A.f1", "yout", "T", "A.f4", "A.f3", "Zc", "Z.go", "Z.m0", "Z.m1",
    "Z.swap", "B.first", "Zr", "B.f2", "B.f1", "B.f0", "B.f3", "B.f4", "Pc", "P.go", "P.m1", "P.m0", "Pr", "Wc",
    "W.go", "W.m1", "W.m0", "W.swap", "Wr", "G.first", "G.f0", "G.f1", "Oc", "Ol", "osw", "osum", "O.first",
    "O.f2", "O.f1", "O.f0", "O.f4", "O.f3",
)
order = (
    0, 1, 2, 16, 32, 33, 3, 4, 5, 6, 7, 48, 64, 80, 96, 112, 81, 49, 113, 114, 128, 144, 34, 35, 65, 160, 176,
    66, 82, 50, 36, 67, 83, 51, 37, 192, 208, 161, 146, 130, 177, 84, 52, 224, 53, 193, 131, 147, 209, 69, 85,
    162, 68, 178, 225, 133, 149, 240, 241, 163, 179, 256, 210, 194, 165, 181, 211, 195, 272, 257, 288, 226, 273,
    304, 242, 289, 213, 197, 305, 227, 164, 180, 115, 320, 229, 258, 336, 290, 212, 196, 306, 274, 228, 259,
    337, 321, 261, 338, 260, 322, 352, 368, 353, 369, 355, 357, 384, 400, 371, 354, 385, 401, 370, 356, 372,
    416, 432, 448, 403, 387, 417, 402, 386, 433, 449, 388, 404, 464, 480, 419, 435, 451, 420, 436, 481, 465,
    418, 434, 483, 373, 496, 450, 467, 452, 497, 405, 389, 512, 528, 466, 421, 482, 437, 513, 529, 544, 453,
    499, 560, 468, 484, 561, 545, 498, 515, 531, 576, 469, 485, 577, 514, 530, 563, 547, 500, 501, 562, 546,
    516, 532, 517, 533, 578, 579, 548, 564, 549, 565, 580, 592, 593, 594, 595, 596, 597, 608, 609, 610, 611,
    612, 613, 624, 640, 625, 641, 626, 642, 656, 672, 627, 643, 689, 673, 628, 644, 674, 658, 629, 645, 675,
    659, 688, 657, 692, 676, 690, 677, 661, 691, 704, 720, 660, 722, 706, 693, 707, 723, 709, 725,
)


def device(yh, z, yl, x, c):
    return (yh * 4 + z, yl * 8 + x * 2 + c)


def remote(src, dst, s, r, dest):
    return pltpu.make_async_remote_copy(src, dst, s, r, device_id=dest, device_id_type=MESH)


class Gather:
    def __init__(self, part, ways, ssem, rsem, p, q, to):
        self.part, self.ways, self.ssem, self.rsem, self.p, self.q, self.to = part, ways, ssem, rsem, p, q, to

    def plan(self, j):
        p, q = self.p, self.q
        o, r, l, a = 1 - p, (q + 1) % 4, (q + 3) % 4, (q + 2) % 4
        if self.ways[j] == "r":
            return (
                ((p, q, None), (p, r), (p, l, None)),
                ((p, q, None), (p, l), (p, r, None)),
                ((p, l, 0), (p, r), (p, a, 0)),
                ((p, r, 1), (p, l), (p, a, 1)),
            )
        if self.ways[j] == "y":
            return (
                ((p, q, None), (o, q), (o, q, None)),
                ((p, q, None), (p, r), (p, l, None)),
                ((p, q, None), (p, l), (p, r, None)),
                ((o, q, None), (p, r), (o, l, None)),
                ((o, q, None), (p, l), (o, r, None)),
                ((p, l, 0), (p, r), (p, a, 0)),
                ((p, r, 1), (p, l), (p, a, 1)),
                ((o, l, 0), (p, r), (o, a, 0)),
                ((o, r, 1), (p, l), (o, a, 1)),
            )
        return (
            ((p, q, None), (p, r), (p, l, None)),
            ((p, q, None), (p, l), (p, r, None)),
            ((p, l, 0), (p, r), (p, a, 0)),
            ((p, r, 1), (p, l), (p, a, 1)),
            ((p, q, None), (o, q), (o, q, None)),
            ((p, l, None), (o, q), (o, l, None)),
            ((p, r, None), (o, q), (o, r, None)),
            ((p, a, None), (o, q), (o, a, None)),
        )

    def copy(self, j, k):
        block, dest, _ = self.plan(j)[k]
        ref = self.part(j, *block)
        return remote(ref, ref, self.ssem.at[j, k], self.rsem.at[j, k], self.to(*dest))

    def start(self, j, *ks):
        for k in ks:
            self.copy(j, k).start()

    def got(self, j, *ks):
        for k in ks:
            _, dest, block = self.plan(j)[k]
            ref = self.part(j, *block)
            remote(ref, ref, self.ssem.at[j, k], self.rsem.at[j, k], self.to(*dest)).wait_recv()

    def step(self, what, j):
        if self.ways[j] == "r":
            waits, starts = {
                "first": ((), (0, 1)),
                "f0": ((0,), (2,)),
                "f1": ((1,), (3,)),
                "last": ((2, 3), ()),
            }[what]
        elif self.ways[j] == "y":
            waits, starts = {
                "first": ((), (0, 1, 2)),
                "f0": ((0,), (3, 4)),
                "f1": ((1,), (5,)),
                "f2": ((2,), (6,)),
                "f3": ((3,), (7,)),
                "f4": ((4,), (8,)),
                "last": ((5, 6, 7, 8), ()),
            }[what]
        else:
            waits, starts = {
                "first": ((), (0, 1, 4)),
                "f0": ((0,), (2, 5)),
                "f1": ((1,), (3, 6)),
                "f2": ((2, 3), (7,)),
                "last": ((4, 5, 6, 7), ()),
            }[what]
        self.got(j, *waits)
        self.start(j, *starts)

    def sent(self):
        for j in range(len(self.ways)):
            for k in range(len(self.plan(j))):
                self.copy(j, k).wait_send()


class Reduce:
    def __init__(self, src, bufs, sems, p, q, to, how):
        self.src, self.p, self.q, self.to, self.how = src, p, q, to, how
        self.mid, self.end = bufs[:2]
        self.ssem, self.rsem = sems[:2]
        if how != "ring":
            self.out, self.got = bufs[2:]
            self.psem, self.qsem = sems[2:]

    def copy(self, j, k):
        q = self.q
        r, l, a = (q + 1) % 4, (q + 3) % 4, (q + 2) % 4
        right, left = self.to(self.p, r), self.to(self.p, l)
        src, dst, dest = (
            (self.src.at[j, a, 0], self.mid.at[j, 0], right),
            (self.src.at[j, a, 1], self.mid.at[j, 1], left),
            (self.src.at[j, r, 1], self.end.at[j, 0, 1], right),
            (self.src.at[j, l, 0], self.end.at[j, 1, 0], left),
            (self.src.at[j, r, 0], self.end.at[j, 0, 0], right),
            (self.src.at[j, l, 1], self.end.at[j, 1, 1], left),
        )[k]
        return remote(src, dst, self.ssem.at[j, k], self.rsem.at[j, k], dest)

    def pair(self, j):
        return remote(
            self.out.at[j], self.got.at[j], self.psem.at[j], self.qsem.at[j], self.to(1 - self.p, self.q)
        )

    def total(self, j, h):
        return (
            self.src[j, self.q, h].astype(f32) + self.end[j, 0, h].astype(f32) + self.end[j, 1, h].astype(f32)
        )

    def step(self, what, j):
        if what == "go":
            for k in range(4):
                self.copy(j, k).start()
        elif what == "swap":
            self.ends(j)
            if self.how == "both":
                for h in range(2):
                    self.out[j, h] = self.total(j, h).astype(bf16)
            else:
                self.out[j] = self.total(j, 1 - self.p).astype(bf16)
            self.pair(j).start()
        else:
            h = 0 if what == "m0" else 1
            t = (self.q + 1 + 2 * h) % 4
            self.copy(j, h).wait_recv()
            self.src[j, t, h] = self.src[j, t, h] + self.mid[j, h]
            self.copy(j, 4 + h).start()

    def ends(self, j):
        for k in range(2, 6):
            self.copy(j, k).wait_recv()

    def result(self, j):
        self.pair(j).wait_recv()
        if self.how == "both":
            return [self.total(j, h) + self.got[j, h].astype(f32) for h in range(2)]
        return self.total(j, self.p) + self.got[j].astype(f32)

    def sent(self, j):
        for k in range(6):
            self.copy(j, k).wait_send()
        if self.how != "ring":
            self.pair(j).wait_send()


def kernel(
    a_ref, g_ref, bi_ref, bo_ref, ein_ref, eout_ref, o_ref,
    am, ag, ym, zp, zfull, big, pp, sc, bo, bot, wg, acc, fs, fr, os, og, es,
    z1, z2, z3, z4, p1, p2, w1, w2, w3, w4,
    lsem, gsem, bsem, tsem,
    a_s, a_r, b_s, b_r, w_s, w_r, o_s, o_r,
    zs, zr, zps, zpr, ps, pr, xs, xr, xps, xpr, sib_s, sib_r, zsib_s, zsib_r, fsib_s, fsib_r, osw_s, osw_r,
):
    rep = lax.axis_index("dp")
    own = lax.axis_index("owner")
    yh, z = rep // 4, rep % 4
    yl, x, c = own // 8, (own // 2) % 4, own % 2
    m = yl * 4 + x
    oc = 1 - c

    sibling = device(yh, z, yl, x, oc)
    over_owner = lambda p, q: device(yh, z, p, q, c)
    over_dp = lambda p, q: device(p, q, yl, x, c)

    barrier = pltpu.get_barrier_semaphore()
    partners = [sibling, over_dp(1 - yh, z), over_owner(1 - yl, x)]
    partners += [over_owner(yl, (x + d) % 4) for d in (1, 3)]
    partners += [over_dp(yh, (z + d) % 4) for d in (1, 3)]
    for dest in partners:
        pl.semaphore_signal(barrier, inc=1, device_id=dest, device_id_type=MESH)

    def at(start, size, step):
        return pl.ds(pl.multiple_of(start, step), size)

    def wide(k):
        return at(k * 768, 768, 768)

    def halves(h, n):
        return pl.ds(0, n) if h is None else pl.ds(h * (n // 2), n // 2)

    def bo_chunk(k):
        return pltpu.make_async_copy(bo_ref.at[wide(k)], bo.at[wide(k)], bsem.at[k])

    def g_chunk(k):
        b = k % 4
        return pltpu.make_async_copy(g_ref.at[:, :, :, wide(k)], zp.at[:, b], gsem.at[b])

    def bi_chunk(j, h):
        dst = big.at[:, at(j * 128 + m * 16, 16, 16), pl.ds(h * 768, 768)]
        return pltpu.make_async_copy(bi_ref.at[j, :, yh, :, wide(h * 4 + z)], dst, tsem.at[j, h])

    load_a = pltpu.make_async_copy(a_ref, am, lsem.at[0])
    load_a.start()
    for k in range(4):
        bo_chunk(k).start()
        g_chunk(k).start()
    for k in range(4, 8):
        bo_chunk(k).start()
    for j in range(b_parts):
        for h in range(2):
            bi_chunk(j, h).start()

    ga = Gather(lambda j, p, q, h: ag.at[j, q, p, halves(h, a_rows)], a_ways, a_s, a_r, yl, x, over_owner)
    gb = Gather(
        lambda j, p, q, h: big.at[halves(h, 4), at(j * 128 + (p * 4 + q) * 16, 16, 16)],
        b_ways, b_s, b_r, yl, x, over_owner,
    )
    gw = Gather(lambda j, p, q, h: wg.at[j, q, halves(h, p_rows)], g_ways, w_s, w_r, yh, z, over_dp)
    go = Gather(lambda j, p, q, h: o_ref.at[p * 4 + q, j, halves(h, o_rows)], o_ways, o_s, o_r, yh, z, over_dp)
    rz = Reduce(zp, (z1, z2, z3, z4), (zs, zr, zps, zpr), yh, z, over_dp, "both")
    rp = Reduce(pp, (p1, p2), (ps, pr), yh, z, over_dp, "ring")
    rw = Reduce(zp, (w1, w2, w3, w4), (xs, xr, xps, xpr), yl, x, over_owner, "split")

    top, half = pl.ds(0, 768), pl.ds(0, 384)
    mine, other = at(c * 384, 384, 128), at(oc * 384, 384, 128)

    def bot_copy(core):
        ref = bot.at[at(core * 384, 384, 128)]
        return remote(ref, ref, sib_s.at[0], sib_r.at[0], sibling)

    send_y = remote(ym.at[:, mine], ym.at[:, mine], sib_s.at[1], sib_r.at[1], sibling)
    tn = (((0,), (0,)), ((), ()))

    lane = lax.broadcasted_iota(jnp.int32, (16, 128), 1)
    place = lax.broadcasted_iota(jnp.int32, (16, 128), 0) + (z * 2 + yh) * 16

    def eigen(_):
        @pl.loop(0, 24)
        def _(i):
            row = ein_ref[pl.ds((2 * (i % 8) + c) * 3 + i // 8, 1), :]
            column = jnp.sum(jnp.where(lane == place, row, 0.0), axis=1, keepdims=True)
            es[at(i * 16, 16, 16), :] = jnp.broadcast_to(column, (16, 128))

    def y_step(k):
        bo_chunk(k).wait()
        g_chunk(k).wait()
        b = k % 4
        lhs = zp[:, b].reshape(768, 768)
        part = jnp.dot(lhs, bo[wide(k), :], preferred_element_type=f32)
        acc[top, half] = part if k == 0 else acc[top, half] + part
        if k + 4 < 8:
            g_chunk(k + 4).start()

    def y_out(_):
        ym[:, mine] = acc[top, half].astype(bf16)
        send_y.start()

    def turn(k):
        rows = pl.ds(k * 1536, 1536)
        bot[mine, rows] = bo[rows, :].T
        if k == 0:
            eigen(k)
        if k == 3:
            bot_copy(c).start()

    def z_part(j):
        if j == 0:
            remote(ym.at[:, other], ym.at[:, other], sib_s.at[1], sib_r.at[1], sibling).wait_recv()
        ga.step("last", j)

        @pl.loop(0, 2)
        def _(t):
            two = pl.ds(2 * t, 2)
            part = jnp.dot(ag[j, two].reshape(4 * a_rows, 768), ym[...], preferred_element_type=f32)
            zp[j, two] = part.astype(bf16).reshape(2, 2, a_rows, 768)

    def z_copy(j, core):
        ref = zfull.at[:, at(core * 384 + j * a_rows, a_rows, a_rows)]
        return remote(ref, ref, zsib_s.at[j], zsib_r.at[j], sibling)

    def z_done(j):
        for h, total in enumerate(rz.result(j)):
            zfull[h, at(c * 384 + j * a_rows, a_rows, a_rows), :] = total.astype(bf16)
        z_copy(j, c).start()

    bi_seen = [0]

    def p_part(j):
        if j == 0:
            for i in range(a_parts):
                z_copy(i, oc).wait_recv()
        while bi_seen[0] * b_rows < (j + 1) * p_rows:
            gb.step("last", bi_seen[0])
            bi_seen[0] += 1
        rows = pl.ds(j * p_rows, p_rows)

        @pl.loop(0, 2)
        def _(t):
            lhs = big[pl.ds(2 * t, 2), rows, :].reshape(2 * p_rows, 1536)
            part = jnp.dot(lhs, zfull[...].reshape(1536, 768), preferred_element_type=f32)
            pp[j, pl.ds(2 * t, 2)] = part.astype(bf16).reshape(2, 2, p_rows // 2, 768)

    def p_done(j):
        rp.ends(j)
        for h in range(2):
            total = rp.total(j, h)
            n = p_rows // 2
            for b in range(6):
                cols = slice(b * 128, (b + 1) * 128)
                scale = es[pl.ds(j * p_rows + h * n, n), :] * eout_ref[pl.ds(m * 6 + b, 1), :] + damping
                sc[j, pl.ds(h * n, n), cols] = (total[:, cols] / scale).astype(bf16)

    def w_part(j):
        if j == 0:
            bot_copy(oc).wait_recv()
            for i in range(a_parts):
                rz.sent(i)

        @pl.loop(0, 8)
        def _(t):
            cols = wide((t % 2) * 4 + t // 2)
            zp[j, t // 2, t % 2] = jnp.dot(sc[j], bot[:, cols], preferred_element_type=f32).astype(bf16)

    def w_done(j):
        wg[j, z] = rw.result(j).astype(bf16)

    def out_part(j):
        gw.step("last", j)
        lhs = big[:, pl.ds(j * p_rows, p_rows), :].reshape(4 * p_rows, 1536)
        part = lax.dot_general(lhs, wg[j].reshape(4 * p_rows, 768), tn, preferred_element_type=f32)
        acc[...] = part if j == 0 else acc[...] + part

    def f_copy(i):
        return remote(fs.at[i], fr.at[i], fsib_s.at[i], fsib_r.at[i], sibling)

    def out_last(i):
        j = p_parts - 1
        if i == 0:
            gw.step("last", j)
        for h in range(2):
            cols = pl.ds(h * 768 + i * o_rows, o_rows)
            lhs = big[:, pl.ds(j * p_rows, p_rows), cols].reshape(4 * p_rows, o_rows)
            part = lax.dot_general(lhs, wg[j].reshape(4 * p_rows, 768), tn, preferred_element_type=f32)
            acc[cols, :] = acc[cols, :] + part
            fs[i, h] = acc[cols, other].astype(bf16)
        f_copy(i).start()

    def o_copy(i):
        return remote(os.at[i], og.at[i], osw_s.at[i], osw_r.at[i], over_dp(1 - yh, z))

    def out_half(i, h):
        return acc[at(h * 768 + i * o_rows, o_rows, o_rows), mine] + fr[i, h].astype(f32)

    def out_swap(i):
        f_copy(i).wait_recv()
        os[i] = out_half(i, 1 - yh).astype(bf16)
        o_copy(i).start()

    def out_sum(i):
        o_copy(i).wait_recv()
        o_ref[rep, i] = (out_half(i, yh) + og[i].astype(f32)).astype(bf16)

    def enter(_):
        load_a.wait()
        for t in range(3):
            per = 128 // a_rows
            ag[pl.ds(t * per, per), x, yl] = am[:, t * 128 : (t + 1) * 128].T.reshape(per, a_rows, 768)
        pl.semaphore_wait(barrier, len(partners))

    others = {
        "Zc": z_part, "Zr": z_done, "Pc": p_part, "Pr": p_done, "Wc": w_part, "Wr": w_done, "Oc": out_part,
        "osw": out_swap, "osum": out_sum, "T": turn, "Y": y_step, "yout": y_out, "bar": enter, "Ol": out_last,
    }
    movers = {"A": ga, "B": gb, "G": gw, "O": go, "Z": rz, "P": rp, "W": rw}

    for step in order:
        name, j = steps[step // 16].split("."), step % 16
        if len(name) == 1:
            others[name[0]](j)
        else:
            if name == ["B", "first"]:
                bi_chunk(j, 0).wait()
                bi_chunk(j, 1).wait()
            movers[name[0]].step(name[1], j)

    for j in range(o_parts):
        go.step("last", j)
    for gather in (ga, gb, gw, go):
        gather.sent()
    for j in range(p_parts):
        rp.sent(j)
        rw.sent(j)
    for i in range(o_parts):
        f_copy(i).wait_send()
        o_copy(i).wait_send()
    bot_copy(c).wait_send()
    send_y.wait_send()
    for j in range(a_parts):
        z_copy(j, c).wait_send()


def shards(activations, out_grads, basis_in, basis_out, eig_in, eig_out):
    dma = pltpu.SemaphoreType.DMA
    v = pltpu.VMEM
    scratch = [
        v((768, 384), bf16), v((a_parts, 4, 2, a_rows, 768), bf16), v((768, 768), bf16),
        v((a_parts, 4, 2, a_rows, 768), bf16), v((2, 768, 768), bf16), v((4, 384, 1536), bf16),
        v((p_parts, 4, 2, p_rows // 2, 768), bf16), v((p_parts, p_rows, 768), bf16), v((6144, 384), bf16),
        v((768, 6144), bf16), v((p_parts, 4, p_rows, 768), bf16), v((1536, 768), f32),
        v((o_parts, 2, o_rows, 384), bf16), v((o_parts, 2, o_rows, 384), bf16), v((o_parts, o_rows, 384), bf16),
        v((o_parts, o_rows, 384), bf16), v((384, 128), f32),
        v((a_parts, 2, a_rows, 768), bf16), v((a_parts, 2, 2, a_rows, 768), bf16),
        v((a_parts, 2, a_rows, 768), bf16), v((a_parts, 2, a_rows, 768), bf16),
        v((p_parts, 2, p_rows // 2, 768), bf16), v((p_parts, 2, 2, p_rows // 2, 768), bf16),
        v((p_parts, 2, p_rows, 768), bf16), v((p_parts, 2, 2, p_rows, 768), bf16), v((p_parts, p_rows, 768), bf16),
        v((p_parts, p_rows, 768), bf16),
    ]
    scratch += [dma((1,)), dma((4,)), dma((8,)), dma((b_parts, 2))]
    for n in (a_parts, b_parts, p_parts, o_parts):
        scratch += [dma((n, 9))] * 2
    scratch += [dma((a_parts, 6))] * 2 + [dma((a_parts,))] * 2 + [dma((p_parts, 6))] * 4 + [dma((p_parts,))] * 2
    scratch += [dma((2,))] * 2 + [dma((a_parts,))] * 2 + [dma((o_parts,))] * 4
    hbm = pl.BlockSpec(memory_space=pl.ANY)
    vmem = pl.BlockSpec(memory_space=pltpu.VMEM)
    out = pl.pallas_call(
        kernel,
        out_shape=pltpu.VMEM((8, o_parts, o_rows, 384), bf16),
        in_specs=[hbm, hbm, hbm, hbm, vmem, vmem],
        out_specs=vmem,
        scratch_shapes=scratch,
        compiler_params=pltpu.CompilerParams(
            collective_id=0, has_side_effects=True, vmem_limit_bytes=59 * 2**20
        ),
        name="precondition",
    )(
        activations, out_grads.reshape(p_parts, 2, p_rows, 6144), basis_in.reshape(b_parts, 4, 2, 16, 6144), basis_out,
        eig_in.reshape(48, 128), eig_out.reshape(48, 128),
    )
    return out.reshape(6144, 384)


def solution(mesh):
    in_specs = (P("dp", "owner"), P("dp", None), P("owner", None), P(None, "owner"), P(), P())
    out_specs = P(None, "owner")
    return jax.shard_map(shards, mesh=mesh, in_specs=in_specs, out_specs=out_specs, check_vma=False)
```

```python
import jax
import jax.numpy as jnp
from jax import lax
from jax.experimental import pallas as pl
from jax.experimental.pallas import tpu as pltpu
from jax.sharding import PartitionSpec as P

damping = 0.1
bf16 = jnp.bfloat16
f32 = jnp.float32
MESH = pl.DeviceIdType.MESH
a_parts, p_parts, b_parts, o_parts = 6, 6, 3, 6
a_rows, p_rows, b_rows, o_rows = 384 // a_parts, 384 // p_parts, 384 // b_parts, 768 // o_parts
a_ways, b_ways, g_ways, o_ways = 'xyyyyy', 'yyy', 'rrrrrr', 'yxyyxy'
steps = (
    "Y", "bar", "A.first", "A.f0", "A.f1", "A.f2", "yout", "T", "A.f4", "A.f3", "Zc", "Z.go", "Z.m0", "Z.m1",
    "Z.swap", "B.first", "B.f0", "B.f2", "B.f1", "B.f4", "B.f3", "Zr", "Pc", "P.go", "P.m1", "P.m0", "Pr", "Wc",
    "Wd", "We", "W.m1", "W.m0", "W.swap", "Wr", "G.first", "G.f1", "G.f0", "Oc", "Ol", "osw", "osum", "O.first",
    "O.f0", "O.f1", "O.f2", "O.f4", "O.f3",
)
order = (
    0, 16, 32, 33, 1, 2, 3, 48, 64, 34, 4, 5, 6, 65, 49, 80, 35, 7, 81, 96, 112, 113, 114, 115, 129, 145, 50,
    66, 36, 82, 160, 176, 51, 130, 146, 52, 67, 37, 192, 208, 161, 83, 177, 53, 131, 162, 178, 193, 209, 224,
    147, 68, 69, 132, 210, 84, 194, 133, 148, 85, 149, 240, 241, 163, 179, 164, 226, 180, 225, 195, 211, 256,
    196, 212, 257, 165, 272, 181, 289, 273, 227, 228, 197, 213, 229, 305, 321, 304, 339, 337, 338, 320, 340,
    288, 242, 336, 341, 355, 371, 258, 274, 353, 369, 387, 290, 403, 352, 368, 401, 385, 354, 370, 306, 322,
    419, 435, 451, 467, 400, 384, 417, 433, 449, 357, 373, 386, 402, 483, 416, 432, 499, 448, 389, 405, 356,
    372, 497, 465, 481, 418, 434, 450, 515, 404, 480, 388, 496, 513, 420, 531, 436, 498, 482, 421, 437, 464,
    547, 529, 545, 452, 484, 512, 466, 514, 500, 453, 469, 563, 577, 561, 485, 528, 544, 468, 501, 516, 530,
    546, 576, 579, 560, 517, 532, 548, 562, 578, 533, 549, 592, 564, 593, 580, 594, 581, 565, 595, 596, 608,
    609, 610, 611, 612, 624, 625, 613, 626, 627, 628, 629, 640, 656, 641, 657, 642, 658, 643, 659, 644, 660,
    645, 661, 672, 689, 676, 688, 692, 673, 674, 675, 693, 706, 707, 722, 677, 723, 704, 708, 736, 691, 705,
    738, 720, 739, 725, 690, 709, 741,
)


def device(yh, z, yl, x, c):
    return (yh * 4 + z, yl * 8 + x * 2 + c)


def remote(src, dst, s, r, dest):
    return pltpu.make_async_remote_copy(src, dst, s, r, device_id=dest, device_id_type=MESH)


class Gather:
    def __init__(self, part, ways, ssem, rsem, p, q, to):
        self.part, self.ways, self.ssem, self.rsem, self.p, self.q, self.to = part, ways, ssem, rsem, p, q, to

    def plan(self, j):
        p, q = self.p, self.q
        o, r, l, a = 1 - p, (q + 1) % 4, (q + 3) % 4, (q + 2) % 4
        if self.ways[j] == "r":
            return (
                ((p, q, None), (p, r), (p, l, None)),
                ((p, q, None), (p, l), (p, r, None)),
                ((p, l, 0), (p, r), (p, a, 0)),
                ((p, r, 1), (p, l), (p, a, 1)),
            )
        if self.ways[j] == "y":
            return (
                ((p, q, None), (o, q), (o, q, None)),
                ((p, q, None), (p, r), (p, l, None)),
                ((p, q, None), (p, l), (p, r, None)),
                ((o, q, None), (p, r), (o, l, None)),
                ((o, q, None), (p, l), (o, r, None)),
                ((p, l, 0), (p, r), (p, a, 0)),
                ((p, r, 1), (p, l), (p, a, 1)),
                ((o, l, 0), (p, r), (o, a, 0)),
                ((o, r, 1), (p, l), (o, a, 1)),
            )
        return (
            ((p, q, None), (p, r), (p, l, None)),
            ((p, q, None), (p, l), (p, r, None)),
            ((p, l, 0), (p, r), (p, a, 0)),
            ((p, r, 1), (p, l), (p, a, 1)),
            ((p, q, None), (o, q), (o, q, None)),
            ((p, l, None), (o, q), (o, l, None)),
            ((p, r, None), (o, q), (o, r, None)),
            ((p, a, None), (o, q), (o, a, None)),
        )

    def copy(self, j, k):
        block, dest, _ = self.plan(j)[k]
        ref = self.part(j, *block)
        return remote(ref, ref, self.ssem.at[j, k], self.rsem.at[j, k], self.to(*dest))

    def start(self, j, *ks):
        for k in ks:
            self.copy(j, k).start()

    def got(self, j, *ks):
        for k in ks:
            _, dest, block = self.plan(j)[k]
            ref = self.part(j, *block)
            remote(ref, ref, self.ssem.at[j, k], self.rsem.at[j, k], self.to(*dest)).wait_recv()

    def step(self, what, j):
        if self.ways[j] == "r":
            waits, starts = {
                "first": ((), (0, 1)),
                "f0": ((0,), (2,)),
                "f1": ((1,), (3,)),
                "last": ((2, 3), ()),
            }[what]
        elif self.ways[j] == "y":
            waits, starts = {
                "first": ((), (0, 1, 2)),
                "f0": ((0,), (3, 4)),
                "f1": ((1,), (5,)),
                "f2": ((2,), (6,)),
                "f3": ((3,), (7,)),
                "f4": ((4,), (8,)),
                "last": ((5, 6, 7, 8), ()),
            }[what]
        else:
            waits, starts = {
                "first": ((), (0, 1, 4)),
                "f0": ((0,), (2, 5)),
                "f1": ((1,), (3, 6)),
                "f2": ((2, 3), (7,)),
                "last": ((4, 5, 6, 7), ()),
            }[what]
        self.got(j, *waits)
        self.start(j, *starts)

    def sent(self):
        for j in range(len(self.ways)):
            for k in range(len(self.plan(j))):
                self.copy(j, k).wait_send()


class Reduce:
    def __init__(self, src, bufs, sems, p, q, to, how):
        self.src, self.p, self.q, self.to, self.how = src, p, q, to, how
        self.mid, self.end = bufs[:2]
        self.ssem, self.rsem = sems[:2]
        if how != "ring":
            self.out, self.got = bufs[2:]
            self.psem, self.qsem = sems[2:]

    def copy(self, j, k):
        q = self.q
        r, l, a = (q + 1) % 4, (q + 3) % 4, (q + 2) % 4
        right, left = self.to(self.p, r), self.to(self.p, l)
        src, dst, dest = (
            (self.src.at[j, a, 0], self.mid.at[j, 0], right),
            (self.src.at[j, a, 1], self.mid.at[j, 1], left),
            (self.src.at[j, r, 1], self.end.at[j, 0, 1], right),
            (self.src.at[j, l, 0], self.end.at[j, 1, 0], left),
            (self.src.at[j, r, 0], self.end.at[j, 0, 0], right),
            (self.src.at[j, l, 1], self.end.at[j, 1, 1], left),
        )[k]
        return remote(src, dst, self.ssem.at[j, k], self.rsem.at[j, k], dest)

    def pair(self, j):
        return remote(
            self.out.at[j], self.got.at[j], self.psem.at[j], self.qsem.at[j], self.to(1 - self.p, self.q)
        )

    def total(self, j, h):
        return (
            self.src[j, self.q, h].astype(f32) + self.end[j, 0, h].astype(f32) + self.end[j, 1, h].astype(f32)
        )

    def step(self, what, j):
        if what == "go":
            self.far(j)
            self.near(j)
        elif what == "swap":
            self.ends(j)
            if self.how == "both":
                for h in range(2):
                    self.out[j, h] = self.total(j, h).astype(bf16)
            else:
                self.out[j] = self.total(j, 1 - self.p).astype(bf16)
            self.pair(j).start()
        else:
            h = 0 if what == "m0" else 1
            t = (self.q + 1 + 2 * h) % 4
            self.copy(j, h).wait_recv()
            self.src[j, t, h] = self.src[j, t, h] + self.mid[j, h]
            self.copy(j, 4 + h).start()

    def far(self, j):
        self.copy(j, 0).start()
        self.copy(j, 1).start()

    def near(self, j):
        self.copy(j, 2).start()
        self.copy(j, 3).start()

    def ends(self, j):
        for k in range(2, 6):
            self.copy(j, k).wait_recv()

    def result(self, j):
        self.pair(j).wait_recv()
        if self.how == "both":
            return [self.total(j, h) + self.got[j, h].astype(f32) for h in range(2)]
        return self.total(j, self.p) + self.got[j].astype(f32)

    def sent(self, j):
        for k in range(6):
            self.copy(j, k).wait_send()
        if self.how != "ring":
            self.pair(j).wait_send()


def kernel(
    a_ref, g_ref, bi_ref, bo_ref, ein_ref, eout_ref, o_ref,
    am, ag, ym, zp, zfull, big, pp, sc, bo, bot, wg, acc, fs, fr, os, og, es,
    z1, z2, z3, z4, p1, p2, w1, w2, w3, w4,
    lsem, gsem, bsem, tsem,
    a_s, a_r, b_s, b_r, w_s, w_r, o_s, o_r,
    zs, zr, zps, zpr, ps, pr, xs, xr, xps, xpr, sib_s, sib_r, zsib_s, zsib_r, fsib_s, fsib_r, osw_s, osw_r,
):
    rep = lax.axis_index("dp")
    own = lax.axis_index("owner")
    yh, z = rep // 4, rep % 4
    yl, x, c = own // 8, (own // 2) % 4, own % 2
    m = yl * 4 + x
    oc = 1 - c

    sibling = device(yh, z, yl, x, oc)
    over_owner = lambda p, q: device(yh, z, p, q, c)
    over_dp = lambda p, q: device(p, q, yl, x, c)

    barrier = pltpu.get_barrier_semaphore()
    partners = [sibling, over_dp(1 - yh, z), over_owner(1 - yl, x)]
    partners += [over_owner(yl, (x + d) % 4) for d in (1, 3)]
    partners += [over_dp(yh, (z + d) % 4) for d in (1, 3)]
    for dest in partners:
        pl.semaphore_signal(barrier, inc=1, device_id=dest, device_id_type=MESH)

    def at(start, size, step):
        return pl.ds(pl.multiple_of(start, step), size)

    def wide(k):
        return at(k * 768, 768, 768)

    def halves(h, n):
        return pl.ds(0, n) if h is None else pl.ds(h * (n // 2), n // 2)

    def bo_chunk(k):
        return pltpu.make_async_copy(bo_ref.at[wide(k)], bo.at[wide(k)], bsem.at[k])

    def g_chunk(k):
        b = k % 4
        return pltpu.make_async_copy(g_ref.at[:, :, :, wide(k)], zp.at[:, b], gsem.at[b])

    def bi_chunk(j, h):
        dst = big.at[:, at(j * 128 + m * 16, 16, 16), pl.ds(h * 768, 768)]
        return pltpu.make_async_copy(bi_ref.at[j, :, yh, :, wide(h * 4 + z)], dst, tsem.at[j, h])

    load_a = pltpu.make_async_copy(a_ref, am, lsem.at[0])
    load_a.start()
    for k in range(4):
        bo_chunk(k).start()
        g_chunk(k).start()
    for k in range(4, 8):
        bo_chunk(k).start()
    for j in range(b_parts):
        for h in range(2):
            bi_chunk(j, h).start()

    ga = Gather(lambda j, p, q, h: ag.at[j, q, p, halves(h, a_rows)], a_ways, a_s, a_r, yl, x, over_owner)
    gb = Gather(
        lambda j, p, q, h: big.at[halves(h, 4), at(j * 128 + (p * 4 + q) * 16, 16, 16)],
        b_ways, b_s, b_r, yl, x, over_owner,
    )
    gw = Gather(lambda j, p, q, h: wg.at[j, q, halves(h, p_rows)], g_ways, w_s, w_r, yh, z, over_dp)
    go = Gather(lambda j, p, q, h: o_ref.at[p * 4 + q, j, halves(h, o_rows)], o_ways, o_s, o_r, yh, z, over_dp)
    rz = Reduce(zp, (z1, z2, z3, z4), (zs, zr, zps, zpr), yh, z, over_dp, "both")
    rp = Reduce(pp, (p1, p2), (ps, pr), yh, z, over_dp, "ring")
    rw = Reduce(zp, (w1, w2, w3, w4), (xs, xr, xps, xpr), yl, x, over_owner, "split")

    top, half = pl.ds(0, 768), pl.ds(0, 384)
    mine, other = at(c * 384, 384, 128), at(oc * 384, 384, 128)

    def bot_copy(core):
        ref = bot.at[at(core * 384, 384, 128)]
        return remote(ref, ref, sib_s.at[0], sib_r.at[0], sibling)

    send_y = remote(ym.at[:, mine], ym.at[:, mine], sib_s.at[1], sib_r.at[1], sibling)
    tn = (((0,), (0,)), ((), ()))

    lane = lax.broadcasted_iota(jnp.int32, (16, 128), 1)
    place = lax.broadcasted_iota(jnp.int32, (16, 128), 0) + (z * 2 + yh) * 16

    def eigen():
        @pl.loop(0, 24)
        def _(i):
            row = ein_ref[pl.ds((2 * (i % 8) + c) * 3 + i // 8, 1), :]
            column = jnp.sum(jnp.where(lane == place, row, 0.0), axis=1, keepdims=True)
            es[at(i * 16, 16, 16), :] = jnp.broadcast_to(column, (16, 128))

    done = set()

    def once(name):
        first = name not in done
        done.add(name)
        return first

    def y_step(k):
        bo_chunk(k).wait()
        g_chunk(k).wait()
        b = k % 4
        lhs = zp[:, b].reshape(768, 768)
        part = jnp.dot(lhs, bo[wide(k), :], preferred_element_type=f32)
        acc[top, half] = part if k == 0 else acc[top, half] + part
        if k + 4 < 8:
            g_chunk(k + 4).start()

    def y_out(_):
        ym[:, mine] = acc[top, half].astype(bf16)
        send_y.start()
        eigen()

    def turn(k):
        rows = pl.ds(k * 1536, 1536)
        bot[mine, rows] = bo[rows, :].T
        if k == 3:
            bot_copy(c).start()

    def z_part(j):
        if once("Z"):
            remote(ym.at[:, other], ym.at[:, other], sib_s.at[1], sib_r.at[1], sibling).wait_recv()
        ga.step("last", j)

        @pl.loop(0, 2)
        def _(t):
            two = pl.ds(2 * t, 2)
            part = jnp.dot(ag[j, two].reshape(4 * a_rows, 768), ym[...], preferred_element_type=f32)
            zp[j, two] = part.astype(bf16).reshape(2, 2, a_rows, 768)

    def z_copy(j, core):
        ref = zfull.at[:, at(core * 384 + j * a_rows, a_rows, a_rows)]
        return remote(ref, ref, zsib_s.at[j], zsib_r.at[j], sibling)

    def z_done(j):
        for h, total in enumerate(rz.result(j)):
            zfull[h, at(c * 384 + j * a_rows, a_rows, a_rows), :] = total.astype(bf16)
        z_copy(j, c).start()

    bi_seen = [0]

    def p_part(j):
        if once("P"):
            for i in range(a_parts):
                z_copy(i, oc).wait_recv()
        while bi_seen[0] * b_rows < (j + 1) * p_rows:
            gb.step("last", bi_seen[0])
            bi_seen[0] += 1
        rows = pl.ds(j * p_rows, p_rows)

        @pl.loop(0, 2)
        def _(t):
            lhs = big[pl.ds(2 * t, 2), rows, :].reshape(2 * p_rows, 1536)
            part = jnp.dot(lhs, zfull[...].reshape(1536, 768), preferred_element_type=f32)
            pp[j, pl.ds(2 * t, 2)] = part.astype(bf16).reshape(2, 2, p_rows // 2, 768)

    def p_done(j):
        rp.ends(j)
        for h in range(2):
            total = rp.total(j, h)
            n = p_rows // 2
            for b in range(6):
                cols = slice(b * 128, (b + 1) * 128)
                scale = es[pl.ds(j * p_rows + h * n, n), :] * eout_ref[pl.ds(m * 6 + b, 1), :] + damping
                sc[j, pl.ds(h * n, n), cols] = (total[:, cols] / scale).astype(bf16)

    def w_part(j):
        if once("W"):
            bot_copy(oc).wait_recv()
            for i in range(a_parts):
                rz.sent(i)

        w_block(j, (x + 2) % 4)
        rw.far(j)

    def w_block(j, t):
        @pl.loop(0, 2)
        def _(h):
            zp[j, t, h] = jnp.dot(sc[j], bot[:, wide(h * 4 + t)], preferred_element_type=f32).astype(bf16)

    def w_near(j):
        w_block(j, (x + 1) % 4)
        w_block(j, (x + 3) % 4)
        rw.near(j)

    def w_own(j):
        w_block(j, x)

    def w_done(j):
        wg[j, z] = rw.result(j).astype(bf16)

    def out_part(j):
        gw.step("last", j)
        lhs = big[:, pl.ds(j * p_rows, p_rows), :].reshape(4 * p_rows, 1536)
        part = lax.dot_general(lhs, wg[j].reshape(4 * p_rows, 768), tn, preferred_element_type=f32)
        acc[...] = part if j == 0 else acc[...] + part

    def f_copy(i):
        return remote(fs.at[i], fr.at[i], fsib_s.at[i], fsib_r.at[i], sibling)

    def out_last(i):
        j = p_parts - 1
        if i == 0:
            gw.step("last", j)
        for h in range(2):
            cols = pl.ds(h * 768 + i * o_rows, o_rows)
            lhs = big[:, pl.ds(j * p_rows, p_rows), cols].reshape(4 * p_rows, o_rows)
            part = lax.dot_general(lhs, wg[j].reshape(4 * p_rows, 768), tn, preferred_element_type=f32)
            acc[cols, :] = acc[cols, :] + part
            fs[i, h] = acc[cols, other].astype(bf16)
        f_copy(i).start()

    def o_copy(i):
        return remote(os.at[i], og.at[i], osw_s.at[i], osw_r.at[i], over_dp(1 - yh, z))

    def out_half(i, h):
        return acc[at(h * 768 + i * o_rows, o_rows, o_rows), mine] + fr[i, h].astype(f32)

    def out_swap(i):
        f_copy(i).wait_recv()
        os[i] = out_half(i, 1 - yh).astype(bf16)
        o_copy(i).start()

    def out_sum(i):
        o_copy(i).wait_recv()
        o_ref[rep, i] = (out_half(i, yh) + og[i].astype(f32)).astype(bf16)

    def enter(_):
        load_a.wait()
        for t in range(3):
            per = 128 // a_rows
            ag[pl.ds(t * per, per), x, yl] = am[:, t * 128 : (t + 1) * 128].T.reshape(per, a_rows, 768)
        pl.semaphore_wait(barrier, len(partners))

    others = {
        "Zc": z_part, "Zr": z_done, "Pc": p_part, "Pr": p_done, "Wc": w_part, "Wd": w_near, "We": w_own, "Wr": w_done, "Oc": out_part,
        "osw": out_swap, "osum": out_sum, "T": turn, "Y": y_step, "yout": y_out, "bar": enter, "Ol": out_last,
    }
    movers = {"A": ga, "B": gb, "G": gw, "O": go, "Z": rz, "P": rp, "W": rw}

    for step in order:
        name, j = steps[step // 16].split("."), step % 16
        if len(name) == 1:
            others[name[0]](j)
        else:
            if name == ["B", "first"]:
                bi_chunk(j, 0).wait()
                bi_chunk(j, 1).wait()
            movers[name[0]].step(name[1], j)

    for j in range(o_parts):
        go.step("last", j)
    for gather in (ga, gb, gw, go):
        gather.sent()
    for j in range(p_parts):
        rp.sent(j)
        rw.sent(j)
    for i in range(o_parts):
        f_copy(i).wait_send()
        o_copy(i).wait_send()
    bot_copy(c).wait_send()
    send_y.wait_send()
    for j in range(a_parts):
        z_copy(j, c).wait_send()


def shards(activations, out_grads, basis_in, basis_out, eig_in, eig_out):
    dma = pltpu.SemaphoreType.DMA
    v = pltpu.VMEM
    scratch = [
        v((768, 384), bf16), v((a_parts, 4, 2, a_rows, 768), bf16), v((768, 768), bf16),
        v((a_parts, 4, 2, a_rows, 768), bf16), v((2, 768, 768), bf16), v((4, 384, 1536), bf16),
        v((p_parts, 4, 2, p_rows // 2, 768), bf16), v((p_parts, p_rows, 768), bf16), v((6144, 384), bf16),
        v((768, 6144), bf16), v((p_parts, 4, p_rows, 768), bf16), v((1536, 768), f32),
        v((o_parts, 2, o_rows, 384), bf16), v((o_parts, 2, o_rows, 384), bf16), v((o_parts, o_rows, 384), bf16),
        v((o_parts, o_rows, 384), bf16), v((384, 128), f32),
        v((a_parts, 2, a_rows, 768), bf16), v((a_parts, 2, 2, a_rows, 768), bf16),
        v((a_parts, 2, a_rows, 768), bf16), v((a_parts, 2, a_rows, 768), bf16),
        v((p_parts, 2, p_rows // 2, 768), bf16), v((p_parts, 2, 2, p_rows // 2, 768), bf16),
        v((p_parts, 2, p_rows, 768), bf16), v((p_parts, 2, 2, p_rows, 768), bf16), v((p_parts, p_rows, 768), bf16),
        v((p_parts, p_rows, 768), bf16),
    ]
    scratch += [dma((1,)), dma((4,)), dma((8,)), dma((b_parts, 2))]
    for n in (a_parts, b_parts, p_parts, o_parts):
        scratch += [dma((n, 9))] * 2
    scratch += [dma((a_parts, 6))] * 2 + [dma((a_parts,))] * 2 + [dma((p_parts, 6))] * 4 + [dma((p_parts,))] * 2
    scratch += [dma((2,))] * 2 + [dma((a_parts,))] * 2 + [dma((o_parts,))] * 4
    hbm = pl.BlockSpec(memory_space=pl.ANY)
    vmem = pl.BlockSpec(memory_space=pltpu.VMEM)
    out = pl.pallas_call(
        kernel,
        out_shape=pltpu.VMEM((8, o_parts, o_rows, 384), bf16),
        in_specs=[hbm, hbm, hbm, hbm, vmem, vmem],
        out_specs=vmem,
        scratch_shapes=scratch,
        compiler_params=pltpu.CompilerParams(
            collective_id=0, has_side_effects=True, vmem_limit_bytes=59 * 2**20
        ),
        name="precondition",
    )(
        activations, out_grads.reshape(p_parts, 2, p_rows, 6144), basis_in.reshape(b_parts, 4, 2, 16, 6144), basis_out,
        eig_in.reshape(48, 128), eig_out.reshape(48, 128),
    )
    return out.reshape(6144, 384)


def solution(mesh):
    in_specs = (P("dp", "owner"), P("dp", None), P("owner", None), P(None, "owner"), P(), P())
    out_specs = P(None, "owner")
    return jax.shard_map(shards, mesh=mesh, in_specs=in_specs, out_specs=out_specs, check_vma=False)
```

```python
import jax
import jax.numpy as jnp
from jax import lax
from jax.experimental import pallas as pl
from jax.experimental.pallas import tpu as pltpu
from jax.sharding import PartitionSpec as P

damping = 0.1
bf16 = jnp.bfloat16
f32 = jnp.float32
MESH = pl.DeviceIdType.MESH
a_parts, p_parts, b_parts, o_parts = 6, 6, 3, 6
a_rows, p_rows, b_rows, o_rows = 384 // a_parts, 384 // p_parts, 384 // b_parts, 768 // o_parts
a_ways, b_ways, g_ways, o_ways = 'xyyyyy', 'yyy', 'rrrrrr', 'yxyyxy'
steps = (
    "Y", "bar", "A.first", "A.f0", "A.f1", "A.f2", "yout", "T", "A.f3", "A.f4", "Zc", "Z.go", "Z.m0", "Z.m1",
    "Z.swap", "B.first", "Zr", "B.f0", "B.f1", "B.f2", "B.f3", "B.f4", "Pc", "P.go", "P.m1", "P.m0", "Pr", "Wc",
    "Wd", "We", "W.m0", "W.m1", "W.swap", "Wr", "G.first", "G.f1", "G.f0", "Oc", "Ol", "osw", "osum", "O.first",
    "O.f2", "O.f1", "O.f0", "O.f3", "O.f4",
)
order = (
    0, 16, 32, 33, 1, 2, 3, 4, 5, 48, 64, 49, 6, 7, 80, 34, 96, 112, 81, 129, 65, 145, 35, 160, 176, 50, 161,
    51, 177, 82, 66, 36, 192, 146, 83, 130, 208, 113, 114, 115, 131, 147, 67, 209, 193, 52, 37, 224, 162, 178,
    225, 53, 163, 179, 132, 84, 148, 68, 85, 69, 149, 133, 240, 241, 194, 210, 195, 211, 164, 180, 165, 181,
    256, 272, 226, 196, 227, 212, 213, 289, 273, 305, 197, 228, 229, 320, 288, 337, 304, 259, 258, 336, 242,
    260, 321, 261, 257, 352, 368, 274, 290, 353, 369, 354, 384, 400, 370, 355, 306, 371, 322, 338, 401, 385,
    416, 432, 448, 387, 403, 402, 386, 417, 433, 449, 465, 357, 419, 435, 451, 480, 496, 356, 372, 464, 499,
    373, 483, 418, 434, 512, 405, 497, 481, 388, 389, 404, 450, 498, 482, 466, 420, 436, 421, 513, 437, 467,
    452, 515, 468, 484, 529, 500, 545, 453, 514, 469, 501, 485, 528, 544, 531, 547, 516, 560, 576, 530, 546,
    517, 561, 577, 532, 548, 562, 578, 563, 533, 549, 592, 579, 593, 594, 580, 564, 581, 565, 595, 596, 608,
    609, 610, 611, 624, 612, 613, 625, 626, 627, 628, 629, 640, 656, 641, 657, 642, 658, 672, 643, 659, 644,
    660, 645, 661, 690, 704, 692, 689, 693, 677, 705, 674, 706, 708, 688, 720, 707, 673, 709, 736, 722, 739,
    741, 723, 691, 738, 725, 675, 676,
)


def device(yh, z, yl, x, c):
    return (yh * 4 + z, yl * 8 + x * 2 + c)


def remote(src, dst, s, r, dest):
    return pltpu.make_async_remote_copy(src, dst, s, r, device_id=dest, device_id_type=MESH)


class Gather:
    def __init__(self, part, ways, ssem, rsem, p, q, to):
        self.part, self.ways, self.ssem, self.rsem, self.p, self.q, self.to = part, ways, ssem, rsem, p, q, to

    def plan(self, j):
        p, q = self.p, self.q
        o, r, l, a = 1 - p, (q + 1) % 4, (q + 3) % 4, (q + 2) % 4
        if self.ways[j] == "r":
            return (
                ((p, q, None), (p, r), (p, l, None)),
                ((p, q, None), (p, l), (p, r, None)),
                ((p, l, 0), (p, r), (p, a, 0)),
                ((p, r, 1), (p, l), (p, a, 1)),
            )
        if self.ways[j] == "y":
            return (
                ((p, q, None), (o, q), (o, q, None)),
                ((p, q, None), (p, r), (p, l, None)),
                ((p, q, None), (p, l), (p, r, None)),
                ((o, q, None), (p, r), (o, l, None)),
                ((o, q, None), (p, l), (o, r, None)),
                ((p, l, 0), (p, r), (p, a, 0)),
                ((p, r, 1), (p, l), (p, a, 1)),
                ((o, l, 0), (p, r), (o, a, 0)),
                ((o, r, 1), (p, l), (o, a, 1)),
            )
        return (
            ((p, q, None), (p, r), (p, l, None)),
            ((p, q, None), (p, l), (p, r, None)),
            ((p, l, 0), (p, r), (p, a, 0)),
            ((p, r, 1), (p, l), (p, a, 1)),
            ((p, q, None), (o, q), (o, q, None)),
            ((p, l, None), (o, q), (o, l, None)),
            ((p, r, None), (o, q), (o, r, None)),
            ((p, a, None), (o, q), (o, a, None)),
        )

    def copy(self, j, k):
        block, dest, _ = self.plan(j)[k]
        ref = self.part(j, *block)
        return remote(ref, ref, self.ssem.at[j, k], self.rsem.at[j, k], self.to(*dest))

    def start(self, j, *ks):
        for k in ks:
            self.copy(j, k).start()

    def got(self, j, *ks):
        for k in ks:
            _, dest, block = self.plan(j)[k]
            ref = self.part(j, *block)
            remote(ref, ref, self.ssem.at[j, k], self.rsem.at[j, k], self.to(*dest)).wait_recv()

    def step(self, what, j):
        if self.ways[j] == "r":
            waits, starts = {
                "first": ((), (0, 1)),
                "f0": ((0,), (2,)),
                "f1": ((1,), (3,)),
                "last": ((2, 3), ()),
            }[what]
        elif self.ways[j] == "y":
            waits, starts = {
                "first": ((), (0, 1, 2)),
                "f0": ((0,), (3, 4)),
                "f1": ((1,), (5,)),
                "f2": ((2,), (6,)),
                "f3": ((3,), (7,)),
                "f4": ((4,), (8,)),
                "last": ((5, 6, 7, 8), ()),
            }[what]
        else:
            waits, starts = {
                "first": ((), (0, 1, 4)),
                "f0": ((0,), (2, 5)),
                "f1": ((1,), (3, 6)),
                "f2": ((2, 3), (7,)),
                "last": ((4, 5, 6, 7), ()),
            }[what]
        self.got(j, *waits)
        self.start(j, *starts)

    def sent(self):
        for j in range(len(self.ways)):
            for k in range(len(self.plan(j))):
                self.copy(j, k).wait_send()


class Reduce:
    def __init__(self, src, bufs, sems, p, q, to, how):
        self.src, self.p, self.q, self.to, self.how = src, p, q, to, how
        self.mid, self.end = bufs[:2]
        self.ssem, self.rsem = sems[:2]
        if how != "ring":
            self.out, self.got = bufs[2:]
            self.psem, self.qsem = sems[2:]

    def copy(self, j, k):
        q = self.q
        r, l, a = (q + 1) % 4, (q + 3) % 4, (q + 2) % 4
        right, left = self.to(self.p, r), self.to(self.p, l)
        src, dst, dest = (
            (self.src.at[j, a, 0], self.mid.at[j, 0], right),
            (self.src.at[j, a, 1], self.mid.at[j, 1], left),
            (self.src.at[j, r, 1], self.end.at[j, 0, 1], right),
            (self.src.at[j, l, 0], self.end.at[j, 1, 0], left),
            (self.src.at[j, r, 0], self.end.at[j, 0, 0], right),
            (self.src.at[j, l, 1], self.end.at[j, 1, 1], left),
        )[k]
        return remote(src, dst, self.ssem.at[j, k], self.rsem.at[j, k], dest)

    def pair(self, j):
        return remote(
            self.out.at[j], self.got.at[j], self.psem.at[j], self.qsem.at[j], self.to(1 - self.p, self.q)
        )

    def total(self, j, h):
        return (
            self.src[j, self.q, h].astype(f32) + self.end[j, 0, h].astype(f32) + self.end[j, 1, h].astype(f32)
        )

    def step(self, what, j):
        if what == "go":
            self.far(j)
            self.near(j)
        elif what == "swap":
            self.ends(j)
            if self.how == "both":
                for h in range(2):
                    self.out[j, h] = self.total(j, h).astype(bf16)
            else:
                self.out[j] = self.total(j, 1 - self.p).astype(bf16)
            self.pair(j).start()
        else:
            h = 0 if what == "m0" else 1
            t = (self.q + 1 + 2 * h) % 4
            self.copy(j, h).wait_recv()
            self.src[j, t, h] = self.src[j, t, h] + self.mid[j, h]
            self.copy(j, 4 + h).start()

    def far(self, j):
        self.copy(j, 0).start()
        self.copy(j, 1).start()

    def near(self, j):
        self.copy(j, 2).start()
        self.copy(j, 3).start()

    def ends(self, j):
        for k in range(2, 6):
            self.copy(j, k).wait_recv()

    def result(self, j):
        self.pair(j).wait_recv()
        if self.how == "both":
            return [self.total(j, h) + self.got[j, h].astype(f32) for h in range(2)]
        return self.total(j, self.p) + self.got[j].astype(f32)

    def sent(self, j):
        for k in range(6):
            self.copy(j, k).wait_send()
        if self.how != "ring":
            self.pair(j).wait_send()


def kernel(
    a_ref, g_ref, bi_ref, bo_ref, ein_ref, eout_ref, o_ref,
    am, ag, ym, zp, zfull, big, pp, sc, bo, bot, wg, acc, fs, fr, os, og, es,
    z1, z2, z3, z4, p1, p2, w1, w2, w3, w4,
    lsem, gsem, bsem, tsem,
    a_s, a_r, b_s, b_r, w_s, w_r, o_s, o_r,
    zs, zr, zps, zpr, ps, pr, xs, xr, xps, xpr, sib_s, sib_r, zsib_s, zsib_r, fsib_s, fsib_r, osw_s, osw_r,
):
    rep = lax.axis_index("dp")
    own = lax.axis_index("owner")
    yh, z = rep // 4, rep % 4
    yl, x, c = own // 8, (own // 2) % 4, own % 2
    m = yl * 4 + x
    oc = 1 - c

    sibling = device(yh, z, yl, x, oc)
    over_owner = lambda p, q: device(yh, z, p, q, c)
    over_dp = lambda p, q: device(p, q, yl, x, c)

    barrier = pltpu.get_barrier_semaphore()
    partners = [sibling, over_dp(1 - yh, z), over_owner(1 - yl, x)]
    partners += [over_owner(yl, (x + d) % 4) for d in (1, 3)]
    partners += [over_dp(yh, (z + d) % 4) for d in (1, 3)]
    for dest in partners:
        pl.semaphore_signal(barrier, inc=1, device_id=dest, device_id_type=MESH)

    def at(start, size, step):
        return pl.ds(pl.multiple_of(start, step), size)

    def wide(k):
        return at(k * 768, 768, 768)

    def halves(h, n):
        return pl.ds(0, n) if h is None else pl.ds(h * (n // 2), n // 2)

    def bo_chunk(k):
        return pltpu.make_async_copy(bo_ref.at[wide(k)], bo.at[wide(k)], bsem.at[k])

    def g_chunk(k):
        b = k % 4
        return pltpu.make_async_copy(g_ref.at[:, :, :, wide(k)], zp.at[:, b], gsem.at[b])

    def bi_chunk(j, h):
        dst = big.at[:, at(j * 128 + m * 16, 16, 16), pl.ds(h * 768, 768)]
        return pltpu.make_async_copy(bi_ref.at[j, :, yh, :, wide(h * 4 + z)], dst, tsem.at[j, h])

    load_a = pltpu.make_async_copy(a_ref, am, lsem.at[0])
    load_a.start()
    for k in range(4):
        bo_chunk(k).start()
        g_chunk(k).start()
    for k in range(4, 8):
        bo_chunk(k).start()
    for j in range(b_parts):
        for h in range(2):
            bi_chunk(j, h).start()

    ga = Gather(lambda j, p, q, h: ag.at[j, q, p, halves(h, a_rows)], a_ways, a_s, a_r, yl, x, over_owner)
    gb = Gather(
        lambda j, p, q, h: big.at[halves(h, 4), at(j * 128 + (p * 4 + q) * 16, 16, 16)],
        b_ways, b_s, b_r, yl, x, over_owner,
    )
    gw = Gather(lambda j, p, q, h: wg.at[j, q, halves(h, p_rows)], g_ways, w_s, w_r, yh, z, over_dp)
    go = Gather(lambda j, p, q, h: o_ref.at[p * 4 + q, j, halves(h, o_rows)], o_ways, o_s, o_r, yh, z, over_dp)
    rz = Reduce(zp, (z1, z2, z3, z4), (zs, zr, zps, zpr), yh, z, over_dp, "both")
    rp = Reduce(pp, (p1, p2), (ps, pr), yh, z, over_dp, "ring")
    rw = Reduce(zp, (w1, w2, w3, w4), (xs, xr, xps, xpr), yl, x, over_owner, "split")

    top, half = pl.ds(0, 768), pl.ds(0, 384)
    mine, other = at(c * 384, 384, 128), at(oc * 384, 384, 128)

    def bot_copy(core):
        ref = bot.at[at(core * 384, 384, 128)]
        return remote(ref, ref, sib_s.at[0], sib_r.at[0], sibling)

    send_y = remote(ym.at[:, mine], ym.at[:, mine], sib_s.at[1], sib_r.at[1], sibling)
    tn = (((0,), (0,)), ((), ()))

    lane = lax.broadcasted_iota(jnp.int32, (16, 128), 1)
    place = lax.broadcasted_iota(jnp.int32, (16, 128), 0) + (z * 2 + yh) * 16

    def eigen():
        @pl.loop(0, 24)
        def _(i):
            row = ein_ref[pl.ds((2 * (i % 8) + c) * 3 + i // 8, 1), :]
            column = jnp.sum(jnp.where(lane == place, row, 0.0), axis=1, keepdims=True)
            es[at(i * 16, 16, 16), :] = jnp.broadcast_to(column, (16, 128))

    done = set()

    def once(name):
        first = name not in done
        done.add(name)
        return first

    def y_step(k):
        bo_chunk(k).wait()
        g_chunk(k).wait()
        b = k % 4
        lhs = zp[:, b].reshape(768, 768)
        part = jnp.dot(lhs, bo[wide(k), :], preferred_element_type=f32)
        acc[top, half] = part if k == 0 else acc[top, half] + part
        if k + 4 < 8:
            g_chunk(k + 4).start()

    def y_out(_):
        ym[:, mine] = acc[top, half].astype(bf16)
        send_y.start()
        eigen()

    def turn(k):
        rows = pl.ds(k * 1536, 1536)
        bot[mine, rows] = bo[rows, :].T
        if k == 3:
            bot_copy(c).start()

    def z_part(j):
        if once("Z"):
            remote(ym.at[:, other], ym.at[:, other], sib_s.at[1], sib_r.at[1], sibling).wait_recv()
        ga.step("last", j)

        @pl.loop(0, 2)
        def _(t):
            two = pl.ds(2 * t, 2)
            part = jnp.dot(ag[j, two].reshape(4 * a_rows, 768), ym[...], preferred_element_type=f32)
            zp[j, two] = part.astype(bf16).reshape(2, 2, a_rows, 768)

    def z_copy(j, core):
        ref = zfull.at[:, at(core * 384 + j * a_rows, a_rows, a_rows)]
        return remote(ref, ref, zsib_s.at[j], zsib_r.at[j], sibling)

    def z_done(j):
        for h, total in enumerate(rz.result(j)):
            zfull[h, at(c * 384 + j * a_rows, a_rows, a_rows), :] = total.astype(bf16)
        z_copy(j, c).start()

    bi_seen = [0]

    def p_part(j):
        if once("P"):
            for i in range(a_parts):
                z_copy(i, oc).wait_recv()
        while bi_seen[0] * b_rows < (j + 1) * p_rows:
            gb.step("last", bi_seen[0])
            bi_seen[0] += 1
        rows = pl.ds(j * p_rows, p_rows)

        @pl.loop(0, 2)
        def _(t):
            lhs = big[pl.ds(2 * t, 2), rows, :].reshape(2 * p_rows, 1536)
            part = jnp.dot(lhs, zfull[...].reshape(1536, 768), preferred_element_type=f32)
            pp[j, pl.ds(2 * t, 2)] = part.astype(bf16).reshape(2, 2, p_rows // 2, 768)

    def p_done(j):
        rp.ends(j)
        for h in range(2):
            total = rp.total(j, h)
            n = p_rows // 2
            for b in range(6):
                cols = slice(b * 128, (b + 1) * 128)
                scale = es[pl.ds(j * p_rows + h * n, n), :] * eout_ref[pl.ds(m * 6 + b, 1), :] + damping
                sc[j, pl.ds(h * n, n), cols] = (total[:, cols] / scale).astype(bf16)

    def w_part(j):
        if once("W"):
            bot_copy(oc).wait_recv()
            for i in range(a_parts):
                rz.sent(i)

        w_block(j, (x + 2) % 4)
        rw.far(j)

    def w_block(j, t):
        @pl.loop(0, 2)
        def _(h):
            zp[j, t, h] = jnp.dot(sc[j], bot[:, wide(h * 4 + t)], preferred_element_type=f32).astype(bf16)

    def w_near(j):
        w_block(j, (x + 1) % 4)
        w_block(j, (x + 3) % 4)
        rw.near(j)

    def w_own(j):
        w_block(j, x)

    def w_done(j):
        wg[j, z] = rw.result(j).astype(bf16)

    def out_part(j):
        gw.step("last", j)
        lhs = big[:, pl.ds(j * p_rows, p_rows), :].reshape(4 * p_rows, 1536)
        part = lax.dot_general(lhs, wg[j].reshape(4 * p_rows, 768), tn, preferred_element_type=f32)
        acc[...] = part if j == 0 else acc[...] + part

    def f_copy(i):
        return remote(fs.at[i], fr.at[i], fsib_s.at[i], fsib_r.at[i], sibling)

    def out_last(i):
        j = p_parts - 1
        if i == 0:
            gw.step("last", j)
        for h in range(2):
            cols = pl.ds(h * 768 + i * o_rows, o_rows)
            lhs = big[:, pl.ds(j * p_rows, p_rows), cols].reshape(4 * p_rows, o_rows)
            part = lax.dot_general(lhs, wg[j].reshape(4 * p_rows, 768), tn, preferred_element_type=f32)
            acc[cols, :] = acc[cols, :] + part
            fs[i, h] = acc[cols, other].astype(bf16)
        f_copy(i).start()

    def o_copy(i):
        return remote(os.at[i], og.at[i], osw_s.at[i], osw_r.at[i], over_dp(1 - yh, z))

    def out_half(i, h):
        return acc[at(h * 768 + i * o_rows, o_rows, o_rows), mine] + fr[i, h].astype(f32)

    def out_swap(i):
        f_copy(i).wait_recv()
        os[i] = out_half(i, 1 - yh).astype(bf16)
        o_copy(i).start()

    def out_sum(i):
        o_copy(i).wait_recv()
        o_ref[rep, i] = (out_half(i, yh) + og[i].astype(f32)).astype(bf16)

    def enter(_):
        load_a.wait()
        for t in range(3):
            per = 128 // a_rows
            ag[pl.ds(t * per, per), x, yl] = am[:, t * 128 : (t + 1) * 128].T.reshape(per, a_rows, 768)
        pl.semaphore_wait(barrier, len(partners))

    others = {
        "Zc": z_part, "Zr": z_done, "Pc": p_part, "Pr": p_done, "Wc": w_part, "Wd": w_near, "We": w_own, "Wr": w_done, "Oc": out_part,
        "osw": out_swap, "osum": out_sum, "T": turn, "Y": y_step, "yout": y_out, "bar": enter, "Ol": out_last,
    }
    movers = {"A": ga, "B": gb, "G": gw, "O": go, "Z": rz, "P": rp, "W": rw}

    for step in order:
        name, j = steps[step // 16].split("."), step % 16
        if len(name) == 1:
            others[name[0]](j)
        else:
            if name == ["B", "first"]:
                bi_chunk(j, 0).wait()
                bi_chunk(j, 1).wait()
            movers[name[0]].step(name[1], j)

    for j in range(o_parts):
        go.step("last", j)
    for gather in (ga, gb, gw, go):
        gather.sent()
    for j in range(p_parts):
        rp.sent(j)
        rw.sent(j)
    for i in range(o_parts):
        f_copy(i).wait_send()
        o_copy(i).wait_send()
    bot_copy(c).wait_send()
    send_y.wait_send()
    for j in range(a_parts):
        z_copy(j, c).wait_send()


def shards(activations, out_grads, basis_in, basis_out, eig_in, eig_out):
    dma = pltpu.SemaphoreType.DMA
    v = pltpu.VMEM
    scratch = [
        v((768, 384), bf16), v((a_parts, 4, 2, a_rows, 768), bf16), v((768, 768), bf16),
        v((a_parts, 4, 2, a_rows, 768), bf16), v((2, 768, 768), bf16), v((4, 384, 1536), bf16),
        v((p_parts, 4, 2, p_rows // 2, 768), bf16), v((p_parts, p_rows, 768), bf16), v((6144, 384), bf16),
        v((768, 6144), bf16), v((p_parts, 4, p_rows, 768), bf16), v((1536, 768), f32),
        v((o_parts, 2, o_rows, 384), bf16), v((o_parts, 2, o_rows, 384), bf16), v((o_parts, o_rows, 384), bf16),
        v((o_parts, o_rows, 384), bf16), v((384, 128), f32),
        v((a_parts, 2, a_rows, 768), bf16), v((a_parts, 2, 2, a_rows, 768), bf16),
        v((a_parts, 2, a_rows, 768), bf16), v((a_parts, 2, a_rows, 768), bf16),
        v((p_parts, 2, p_rows // 2, 768), bf16), v((p_parts, 2, 2, p_rows // 2, 768), bf16),
        v((p_parts, 2, p_rows, 768), bf16), v((p_parts, 2, 2, p_rows, 768), bf16), v((p_parts, p_rows, 768), bf16),
        v((p_parts, p_rows, 768), bf16),
    ]
    scratch += [dma((1,)), dma((4,)), dma((8,)), dma((b_parts, 2))]
    for n in (a_parts, b_parts, p_parts, o_parts):
        scratch += [dma((n, 9))] * 2
    scratch += [dma((a_parts, 6))] * 2 + [dma((a_parts,))] * 2 + [dma((p_parts, 6))] * 4 + [dma((p_parts,))] * 2
    scratch += [dma((2,))] * 2 + [dma((a_parts,))] * 2 + [dma((o_parts,))] * 4
    hbm = pl.BlockSpec(memory_space=pl.ANY)
    vmem = pl.BlockSpec(memory_space=pltpu.VMEM)
    out = pl.pallas_call(
        kernel,
        out_shape=pltpu.VMEM((8, o_parts, o_rows, 384), bf16),
        in_specs=[hbm, hbm, hbm, hbm, vmem, vmem],
        out_specs=vmem,
        scratch_shapes=scratch,
        compiler_params=pltpu.CompilerParams(
            collective_id=0, has_side_effects=True, vmem_limit_bytes=59 * 2**20
        ),
        name="precondition",
    )(
        activations, out_grads.reshape(p_parts, 2, p_rows, 6144), basis_in.reshape(b_parts, 4, 2, 16, 6144), basis_out,
        eig_in.reshape(48, 128), eig_out.reshape(48, 128),
    )
    return out.reshape(6144, 384)


def solution(mesh):
    in_specs = (P("dp", "owner"), P("dp", None), P("owner", None), P(None, "owner"), P(), P())
    out_specs = P(None, "owner")
    return jax.shard_map(shards, mesh=mesh, in_specs=in_specs, out_specs=out_specs, check_vma=False)
```
